32 devices in a mesh: row: 8 (over z, y), col: 4 (over x, core).
Axes of the slice: x: 2, y: 2, z: 4, core: 2. Of those that a mesh axis runs over, the one named last changes fastest.
Arguments:
- trailing_inverse: bfloat16 [2048, 2048], P('row', 'col'), may hold values from -0.125 to 0.125
- l_panel: bfloat16 [2048, 512], P('row', 'col'), may hold values from -6 to 6
- pattern: int32 [8, 2], replicated, may hold values 0 or 1
Outputs:
- inverse_panel: float32 [2048, 512], P('row', 'col')
The draws below stay inside these ranges and needn't reach their ends.
Inputs may be any that keep to these rules, and one draw needn't show every extreme that they name: pattern holds only 0 and 1.
All inputs are finite; a program needn't handle non-finite values.
Results may differ from the reference program's by a relative error of at most 0.0003.
Values may be sent and summed in bfloat16 or wider, within the bound.
A program may use at most 64 MiB of HBM per device.

```python
import jax
import jax.numpy as jnp

B = 256
KS = 2
R = 8


def with_ends(values, stream_key, least, largest):
    place = [jax.random.randint(jax.random.fold_in(stream_key, axis), (), 0, length) for axis, length in enumerate(values.shape)]
    widest = values.shape.index(max(values.shape))
    next_to = place[:widest] + [(place[widest] + 1) % values.shape[widest]] + place[widest + 1:]
    return values.at[tuple(place)].set(least).at[tuple(next_to)].set(largest)


def shard_levels(rng, shape, shards, smallest, high):
    factor_of = 1.0
    for dim, shards_of in shards:
        heights = jax.random.uniform(jax.random.fold_in(jax.random.fold_in(rng, 6), dim), (shards_of,), jnp.float32, smallest / len(shards), high / len(shards))
        factor_of = factor_of * jnp.repeat(jnp.exp(heights), shape[dim] // shards_of).reshape((-1,) + (1,) * (len(shape) - 1 - dim))
    return factor_of


def normal_values(key, extent, width, limit, cuts=(), dtype=jnp.bfloat16):
    drawn = width * jax.random.normal(key, extent, jnp.float32)
    if cuts:
        drawn = drawn * shard_levels(key, extent, cuts, -0.22, 0.18)
    return jnp.clip(drawn, -limit, limit).astype(dtype)


def setup_inputs(seed: int = 0) -> dict:
    splits = jax.random.split(jax.random.key(seed), 4)
    trailing_inverse = normal_values(splits[0], (R * B, R * B), (R * B) ** -0.5, 0.125, ((0, 8), (1, 4)))
    l_panel = normal_values(splits[1], (R * B, KS * B), 1.0, 6.0, ((0, 8), (1, 4)))
    pattern = with_ends((jax.random.randint(splits[2], (R, KS), 0, 2) < 1).astype(jnp.int32), jax.random.fold_in(splits[2], 1), 0, 1)
    return dict(trailing_inverse=trailing_inverse, l_panel=l_panel, pattern=pattern)


def reference(trailing_inverse, l_panel, pattern):
    block_rows, supernodes = pattern.shape
    keep = pattern.astype(jnp.bfloat16)
    masked_panel = (l_panel.reshape(block_rows, B, supernodes, B) * keep[:, None, :, None]).reshape(block_rows * B, supernodes * B)
    product = jnp.dot(trailing_inverse, masked_panel, preferred_element_type=jnp.float32)
    negated = -pattern.astype(jnp.float32)
    result = product.reshape(block_rows, B, supernodes, B) * negated[:, None, :, None]
    return result.reshape(block_rows * B, supernodes * B)
```

```python
import functools

import jax
import jax.numpy as jnp
from jax import lax
from jax.experimental import pallas as pl
from jax.experimental.pallas import tpu as pltpu
from jax.sharding import PartitionSpec as P

B = 256
RB = 1
MESH = pl.DeviceIdType.MESH
T_CHUNKS = 4
P_CHUNKS = 2


def broadcast(value, axis, source):
    kept = jnp.where(lax.axis_index(axis) == source, value, 0).astype(value.dtype)
    return lax.psum(kept, axis)


def per_device(trailing_inverse, l_panel, pattern):
    grid_row = lax.axis_index("row")
    grid_col = lax.axis_index("col")
    ratio = lax.axis_size("row") // lax.axis_size("col")
    local_rows = l_panel.shape[0]
    supernodes = pattern.shape[1]
    my_pattern = lax.dynamic_slice_in_dim(pattern, grid_row * RB, RB, 0)
    full_row = lax.all_gather(l_panel, "col", axis=1, tiled=True)
    keep = my_pattern.astype(jnp.bfloat16)
    masked_row = (full_row.reshape(RB, B, supernodes, B) * keep[:, None, :, None]).reshape(
        local_rows, supernodes * B
    )
    arrived = []
    columns = []
    for turn in range(ratio):
        root = grid_col * ratio + turn
        piece = broadcast(masked_row, "row", root)
        inverse_cols = lax.dynamic_slice_in_dim(trailing_inverse, turn * local_rows, local_rows, 1)
        arrived.append(piece)
        columns.append(inverse_cols)
    stacked_panel = jnp.concatenate(arrived, 0)
    stacked_inverse = jnp.concatenate(columns, 1)
    partial_value = jnp.dot(stacked_inverse, stacked_panel, preferred_element_type=jnp.float32)
    negated = -my_pattern.astype(jnp.float32)
    signed = (partial_value.reshape(RB, B, supernodes, B) * negated[:, None, :, None]).reshape(
        local_rows, supernodes * B
    )
    return lax.psum_scatter(signed, "col", scatter_dimension=1, tiled=True)


def kernel(pattern_ref, t_ref, l_ref, out_ref, t_own, t_far, l_own, l_masked, m, p_send, p_recv,
           load_sem, z_send, c_send, f_send, t_send, t_recv, q_send, q_recv, m_recv):
    row = lax.axis_index("row")
    col = lax.axis_index("col")
    z, y = row // 2, row % 2
    x, k = col // 2, col % 2
    home = z % 2
    is_home = k == home
    rel = (k + home) % 2
    near = (z // 2 + x) % 2

    def at(z_, y_, x_, k_):
        return (z_ * 2 + y_, x_ * 2 + k_)

    def slot(rel_, zrel_, y_):
        rows = pl.ds(pl.multiple_of((zrel_ * 2 + y_) * B, B), B)
        return m.at[rel_, rows], m_recv.at[(rel_ * 2 + zrel_) * 2 + y_]

    def copy(src, dst, send, recv, where):
        return pltpu.make_async_remote_copy(
            src_ref=src, dst_ref=dst, send_sem=send, recv_sem=recv, device_id=where, device_id_type=MESH
        )

    x_mate = at(z, y, 1 - x, k)
    sibling = at(z, y, x, 1 - k)
    y_mate = at(z, 1 - y, x, k)

    load_l = pltpu.make_async_copy(l_ref, l_own, load_sem.at[0])
    load_t = pltpu.make_async_copy(t_ref, t_own, load_sem.at[1])
    load_l.start()
    load_t.start()

    barrier = pltpu.get_barrier_semaphore()

    def greet(where):
        pl.semaphore_signal(barrier, inc=1, device_id=where, device_id_type=MESH)

    greet(x_mate)
    greet(sibling)
    greet(y_mate)
    for zi in range(2):
        @pl.when(2 * zi + k != z)
        def _(zi=zi):
            greet(at(2 * zi + k, y, x, 0))
            greet(at(2 * zi + k, y, x, 1))

    @pl.when(is_home)
    def _():
        greet(at(z, 1 - y, x, 1 - k))

    load_l.wait()
    keep = pattern_ref[row, x].astype(jnp.float32)
    l_masked[...] = (l_own[...].astype(jnp.float32) * keep).astype(jnp.bfloat16)

    @pl.when(is_home)
    def _():
        rows = pl.ds(pl.multiple_of((near * 2 + y) * B, B), B)
        m[0, rows, :] = l_masked[...]

    @pl.when(is_home)
    def _():
        pl.semaphore_wait(barrier, 6)

    @pl.when(jnp.logical_not(is_home))
    def _():
        pl.semaphore_wait(barrier, 7)

    mine, mine_sem = slot(rel, near, y)
    z_copies = [
        copy(l_masked, mine, z_send.at[i], mine_sem, at(z_to, y, x, home))
        for i, z_to in enumerate((3 - z, (z + 2) % 4, z + 1 - 2 * (z % 2)))
    ]
    cross = copy(l_masked, mine, c_send.at[0], mine_sem, at(z, 1 - y, x, home))
    inside = copy(l_masked, mine, c_send.at[1], mine_sem, sibling)
    t_rows = t_far.shape[0] // T_CHUNKS
    t_copies = [
        copy(t_ref.at[pl.ds(i * t_rows, t_rows)], t_far.at[pl.ds(i * t_rows, t_rows)],
             t_send.at[i], t_recv.at[i], x_mate)
        for i in range(T_CHUNKS)
    ]
    for c in z_copies:
        c.start()
    cross.start()

    @pl.when(jnp.logical_not(is_home))
    def _():
        inside.start()

    for c in t_copies:
        c.start()

    forwards = []
    for step, zi in enumerate((z // 2, 1 - z // 2)):
        zrel = (zi + x) % 2
        from_afar = 2 * zi + k != z
        for r in range(2):
            block, sem = slot(r, zrel, y)
            f = copy(block, block, f_send.at[step * 2 + r], sem, y_mate)
            forwards.append((from_afar, f))

            @pl.when(from_afar)
            def _(f=f):
                f.wait_recv()
                f.start()

    @pl.when(is_home)
    def _():
        block, sem = slot(1, near, y)
        copy(block, block, c_send.at[1], sem, sibling).wait_recv()

    for step, zi in enumerate((z // 2, 1 - z // 2)):
        zrel = (zi + x) % 2
        for r in range(2):
            block, sem = slot(r, zrel, 1 - y)
            copy(block, block, f_send.at[0], sem, y_mate).wait_recv()

    load_t.wait()
    for c in t_copies:
        c.wait_recv()
    depth = t_own.shape[1]
    p_rows = out_ref.shape[0] // P_CHUNKS
    swaps = []
    near_m = jnp.concatenate([m[0, :depth, :], m[1, :depth, :]], axis=1)
    far_m = jnp.concatenate([m[0, depth:, :], m[1, depth:, :]], axis=1)
    for i in range(P_CHUNKS):
        rows = pl.ds(i * p_rows, p_rows)
        part = jnp.dot(t_own[rows, :], near_m, preferred_element_type=jnp.float32)
        part += jnp.dot(t_far[rows, :], far_m, preferred_element_type=jnp.float32)
        width = out_ref.shape[1]
        p_send[rows, :] = part[:, width:]
        s = copy(p_send.at[rows], p_recv.at[rows], q_send.at[i], q_recv.at[i], sibling)
        s.start()
        swaps.append(s)
        out_ref[rows, :] = part[:, :width]
    for i in range(P_CHUNKS):
        rows = pl.ds(i * p_rows, p_rows)
        swaps[i].wait_recv()
        out_ref[rows, :] = (out_ref[rows, :] + p_recv[rows, :]) * -keep

    for c in z_copies + [cross] + t_copies + swaps:
        c.wait_send()

    @pl.when(jnp.logical_not(is_home))
    def _():
        inside.wait_send()

    for from_afar, f in forwards:
        @pl.when(from_afar)
        def _(f=f):
            f.wait_send()


def fused(trailing_inverse, l_panel, pattern):
    rows, depth = trailing_inverse.shape
    width = l_panel.shape[1]
    planes = 2
    return pl.pallas_call(
        kernel,
        out_shape=jax.ShapeDtypeStruct((rows, width), jnp.float32),
        in_specs=[
            pl.BlockSpec(memory_space=pltpu.SMEM),
            pl.BlockSpec(memory_space=pl.ANY),
            pl.BlockSpec(memory_space=pl.ANY),
        ],
        out_specs=pl.BlockSpec(memory_space=pltpu.VMEM),
        scratch_shapes=[
            pltpu.VMEM((rows, depth), jnp.bfloat16),
            pltpu.VMEM((rows, depth), jnp.bfloat16),
            pltpu.VMEM((B, width), jnp.bfloat16),
            pltpu.VMEM((B, width), jnp.bfloat16),
            pltpu.VMEM((2, planes * depth, width), jnp.bfloat16),
            pltpu.VMEM((rows, width), jnp.float32),
            pltpu.VMEM((rows, width), jnp.float32),
            pltpu.SemaphoreType.DMA((2,)),
            pltpu.SemaphoreType.DMA((3,)),
            pltpu.SemaphoreType.DMA((2,)),
            pltpu.SemaphoreType.DMA((4,)),
            pltpu.SemaphoreType.DMA((T_CHUNKS,)),
            pltpu.SemaphoreType.DMA((T_CHUNKS,)),
            pltpu.SemaphoreType.DMA((P_CHUNKS,)),
            pltpu.SemaphoreType.DMA((P_CHUNKS,)),
            pltpu.SemaphoreType.DMA((8,)),
        ],
        compiler_params=pltpu.CompilerParams(
            collective_id=0, has_side_effects=True, vmem_limit_bytes=16 * 1024 * 1024
        ),
        cost_estimate=pl.CostEstimate(
            flops=2 * rows * planes * depth * 2 * width, bytes_accessed=rows * depth * 4, transcendentals=0
        ),
    )(pattern, trailing_inverse, l_panel)


def solution(mesh):
    whole_block = (mesh.shape["row"], mesh.shape["col"]) == (8, 4)
    return jax.shard_map(
        fused if whole_block else per_device,
        mesh=mesh,
        in_specs=(P("row", "col"), P("row", "col"), P()),
        out_specs=P("row", "col"),
        check_vma=False,
    )
```

```python
import functools

import jax
import jax.numpy as jnp
from jax import lax
from jax.experimental import pallas as pl
from jax.experimental.pallas import tpu as pltpu
from jax.sharding import PartitionSpec as P

B = 256
RB = 1
MESH = pl.DeviceIdType.MESH
T_CHUNKS = 2
P_CHUNKS = 2


def broadcast(value, axis, source):
    kept = jnp.where(lax.axis_index(axis) == source, value, 0).astype(value.dtype)
    return lax.psum(kept, axis)


def per_device(trailing_inverse, l_panel, pattern):
    grid_row = lax.axis_index("row")
    grid_col = lax.axis_index("col")
    ratio = lax.axis_size("row") // lax.axis_size("col")
    local_rows = l_panel.shape[0]
    supernodes = pattern.shape[1]
    my_pattern = lax.dynamic_slice_in_dim(pattern, grid_row * RB, RB, 0)
    full_row = lax.all_gather(l_panel, "col", axis=1, tiled=True)
    keep = my_pattern.astype(jnp.bfloat16)
    masked_row = (full_row.reshape(RB, B, supernodes, B) * keep[:, None, :, None]).reshape(
        local_rows, supernodes * B
    )
    arrived = []
    columns = []
    for turn in range(ratio):
        root = grid_col * ratio + turn
        piece = broadcast(masked_row, "row", root)
        inverse_cols = lax.dynamic_slice_in_dim(trailing_inverse, turn * local_rows, local_rows, 1)
        arrived.append(piece)
        columns.append(inverse_cols)
    stacked_panel = jnp.concatenate(arrived, 0)
    stacked_inverse = jnp.concatenate(columns, 1)
    partial_value = jnp.dot(stacked_inverse, stacked_panel, preferred_element_type=jnp.float32)
    negated = -my_pattern.astype(jnp.float32)
    signed = (partial_value.reshape(RB, B, supernodes, B) * negated[:, None, :, None]).reshape(
        local_rows, supernodes * B
    )
    return lax.psum_scatter(signed, "col", scatter_dimension=1, tiled=True)


def kernel(pattern_ref, t_ref, l_ref, out_ref, pat, t, m, acc, p_send, p_recv,
           load_sem, z_send, c_send, f_send, t_send, t_recv, q_send, q_recv, m_recv):
    row = lax.axis_index("row")
    col = lax.axis_index("col")
    z, y = row // 2, row % 2
    x, k = col // 2, col % 2
    home = z % 2
    is_home = k == home
    rel = (k + home) % 2
    near = (z // 2 + x) % 2
    far = 1 - near
    half = B // 2

    def at(z_, y_, x_, k_):
        return (z_ * 2 + y_, x_ * 2 + k_)

    def slot(rel_, zrel_, y_, part=None):
        sem = ((rel_ * 2 + zrel_) * 2 + y_) * 2
        if part is None:
            return m.at[rel_, zrel_, y_], m_recv.at[sem]
        return m.at[rel_, zrel_, y_, pl.ds(part * half, half)], m_recv.at[sem + part]

    def copy(src, dst, send, recv, where):
        return pltpu.make_async_remote_copy(
            src_ref=src, dst_ref=dst, send_sem=send, recv_sem=recv, device_id=where, device_id_type=MESH
        )

    x_mate = at(z, y, 1 - x, k)
    sibling = at(z, y, x, 1 - k)
    y_mate = at(z, 1 - y, x, k)
    z_next = z + 1 - 2 * (z % 2)

    barrier = pltpu.get_barrier_semaphore()

    def greet(where):
        pl.semaphore_signal(barrier, inc=1, device_id=where, device_id_type=MESH)

    z_far = 2 * (1 - z // 2) + k
    greet(at(z_far, y, x, 0))
    greet(at(z_far, y, x, 1))
    greet(x_mate)
    greet(y_mate)
    greet(sibling)

    @pl.when(is_home)
    def _():
        greet(at(z, 1 - y, x, 1 - k))

    @pl.when(jnp.logical_not(is_home))
    def _():
        for y_ in range(2):
            for k_ in range(2):
                greet(at(z_next, y_, x, k_))

    load_t = pltpu.make_async_copy(t_ref, t.at[0], load_sem.at[0])
    load_pattern = pltpu.make_async_copy(pattern_ref, pat, load_sem.at[1])
    load_l = pltpu.make_async_copy(l_ref, m.at[0, near, y], load_sem.at[2])
    load_pattern.start()
    load_t.start()

    @pl.when(is_home)
    def _():
        load_l.start()
        pl.semaphore_wait(barrier, 7)

    @pl.when(jnp.logical_not(is_home))
    def _():
        pl.semaphore_wait(barrier, 8)

    z_copies = []
    for part in range(2):
        for i, z_to in enumerate((3 - z, (z + 2) % 4)):
            dst, sem = slot(rel, near, y, part)
            z_copies.append(copy(l_ref.at[pl.ds(part * half, half)], dst, z_send.at[part * 2 + i], sem,
                                 at(z_to, y, x, home)))
    mine, mine_sem = slot(rel, near, y)
    cross = copy(l_ref, mine, c_send.at[0], mine_sem, at(z, 1 - y, x, home))
    inside = copy(l_ref, mine, c_send.at[1], mine_sem, sibling)
    direct = copy(l_ref, mine, c_send.at[2], mine_sem, at(z_next, y, x, home))
    diagonal = copy(l_ref, mine, c_send.at[3], mine_sem, at(z_next, 1 - y, x, home))
    t_rows = t.shape[1] // T_CHUNKS
    t_copies = [
        copy(t_ref.at[pl.ds(i * t_rows, t_rows)], t.at[1, pl.ds(i * t_rows, t_rows)],
             t_send.at[i], t_recv.at[i], x_mate)
        for i in range(T_CHUNKS)
    ]
    z_copies[0].start()
    z_copies[1].start()
    t_copies[0].start()
    cross.start()
    z_copies[2].start()
    z_copies[3].start()
    for c in t_copies[1:]:
        c.start()
    direct.start()
    diagonal.start()

    @pl.when(jnp.logical_not(is_home))
    def _():
        inside.start()

    forwards = []
    for part in range(2):
        for r in range(2):
            block, sem = slot(r, far, y, part)
            f = copy(block, block, f_send.at[part * 2 + r], sem, y_mate)
            f.wait_recv()
            f.start()
            forwards.append(f)

    @pl.when(is_home)
    def _():
        load_l.wait()

    def arrive(*place):
        block, sem = slot(*place)
        copy(block, block, f_send.at[0], sem, y_mate).wait_recv()

    @pl.when(jnp.logical_not(is_home))
    def _():
        arrive(0, near, y)

    arrive(1, near, y)
    arrive(0, near, 1 - y)
    arrive(1, near, 1 - y)
    load_pattern.wait()

    def masked(zrel):
        plane = 2 * ((zrel + x) % 2) + k
        blocks = []
        for y_ in range(2):
            keep = pat[x, plane * 2 + y_].astype(jnp.float32).astype(jnp.bfloat16)
            blocks.append(jnp.concatenate([m[0, zrel, y_], m[1, zrel, y_]], axis=1) * keep)
        return jnp.concatenate(blocks, axis=0)

    load_t.wait()
    for c in t_copies:
        c.wait_recv()
    acc[...] = jnp.dot(t[near], masked(near), preferred_element_type=jnp.float32)
    for part in range(2):
        for r in range(2):
            arrive(r, far, 1 - y, part)
    far_m = masked(far)
    width = out_ref.shape[1]
    p_rows = out_ref.shape[0] // P_CHUNKS
    swaps = []
    for i in range(P_CHUNKS):
        rows = pl.ds(i * p_rows, p_rows)
        total = acc[rows, :] + jnp.dot(t[far, rows, :], far_m, preferred_element_type=jnp.float32)
        p_send[rows, :] = total[:, width:]
        s = copy(p_send.at[rows], p_recv.at[rows], q_send.at[i], q_recv.at[i], sibling)
        s.start()
        swaps.append(s)
        out_ref[rows, :] = total[:, :width]

    for c in z_copies + [cross, direct, diagonal] + t_copies + forwards:
        c.wait_send()

    @pl.when(jnp.logical_not(is_home))
    def _():
        inside.wait_send()

    negated = -pat[x, row].astype(jnp.float32)
    for i in range(P_CHUNKS):
        rows = pl.ds(i * p_rows, p_rows)
        swaps[i].wait_recv()
        out_ref[rows, :] = (out_ref[rows, :] + p_recv[rows, :]) * negated
    for s in swaps:
        s.wait_send()


def fused(trailing_inverse, l_panel, pattern):
    rows, depth = trailing_inverse.shape
    width = l_panel.shape[1]
    return pl.pallas_call(
        kernel,
        out_shape=jax.ShapeDtypeStruct((rows, width), jnp.float32),
        in_specs=[pl.BlockSpec(memory_space=pltpu.HBM)] * 3,
        out_specs=pl.BlockSpec(memory_space=pltpu.VMEM),
        scratch_shapes=[
            pltpu.SMEM(pattern.shape[::-1], jnp.int32),
            pltpu.VMEM((2, rows, depth), jnp.bfloat16),
            pltpu.VMEM((2, 2, 2, B, width), jnp.bfloat16),
            pltpu.VMEM((rows, 2 * width), jnp.float32),
            pltpu.VMEM((rows, width), jnp.float32),
            pltpu.VMEM((rows, width), jnp.float32),
            pltpu.SemaphoreType.DMA((3,)),
            pltpu.SemaphoreType.DMA((4,)),
            pltpu.SemaphoreType.DMA((4,)),
            pltpu.SemaphoreType.DMA((4,)),
            pltpu.SemaphoreType.DMA((T_CHUNKS,)),
            pltpu.SemaphoreType.DMA((T_CHUNKS,)),
            pltpu.SemaphoreType.DMA((P_CHUNKS,)),
            pltpu.SemaphoreType.DMA((P_CHUNKS,)),
            pltpu.SemaphoreType.DMA((16,)),
        ],
        compiler_params=pltpu.CompilerParams(
            collective_id=0, has_side_effects=True, vmem_limit_bytes=66846720
        ),
        cost_estimate=pl.CostEstimate(
            flops=2 * rows * 2 * depth * 2 * width, bytes_accessed=rows * depth * 4, transcendentals=0
        ),
    )(pattern.T, trailing_inverse, l_panel)


def solution(mesh):
    whole_block = (mesh.shape["row"], mesh.shape["col"]) == (8, 4)
    return jax.shard_map(
        fused if whole_block else per_device,
        mesh=mesh,
        in_specs=(P("row", "col"), P("row", "col"), P()),
        out_specs=P("row", "col"),
        check_vma=False,
    )
```

```python
import functools

import jax
import jax.numpy as jnp
from jax import lax
from jax.experimental import pallas as pl
from jax.experimental.pallas import tpu as pltpu
from jax.sharding import PartitionSpec as P

B = 256
RB = 1
MESH = pl.DeviceIdType.MESH
T_CHUNKS = 4


def broadcast(value, axis, source):
    kept = jnp.where(lax.axis_index(axis) == source, value, 0).astype(value.dtype)
    return lax.psum(kept, axis)


def per_device(trailing_inverse, l_panel, pattern):
    grid_row = lax.axis_index("row")
    grid_col = lax.axis_index("col")
    ratio = lax.axis_size("row") // lax.axis_size("col")
    local_rows = l_panel.shape[0]
    supernodes = pattern.shape[1]
    my_pattern = lax.dynamic_slice_in_dim(pattern, grid_row * RB, RB, 0)
    full_row = lax.all_gather(l_panel, "col", axis=1, tiled=True)
    keep = my_pattern.astype(jnp.bfloat16)
    masked_row = (full_row.reshape(RB, B, supernodes, B) * keep[:, None, :, None]).reshape(
        local_rows, supernodes * B
    )
    arrived = []
    columns = []
    for turn in range(ratio):
        root = grid_col * ratio + turn
        piece = broadcast(masked_row, "row", root)
        inverse_cols = lax.dynamic_slice_in_dim(trailing_inverse, turn * local_rows, local_rows, 1)
        arrived.append(piece)
        columns.append(inverse_cols)
    stacked_panel = jnp.concatenate(arrived, 0)
    stacked_inverse = jnp.concatenate(columns, 1)
    partial_value = jnp.dot(stacked_inverse, stacked_panel, preferred_element_type=jnp.float32)
    negated = -my_pattern.astype(jnp.float32)
    signed = (partial_value.reshape(RB, B, supernodes, B) * negated[:, None, :, None]).reshape(
        local_rows, supernodes * B
    )
    return lax.psum_scatter(signed, "col", scatter_dimension=1, tiled=True)


def kernel(pattern_ref, t_ref, l_ref, out_ref, pat, t, m, acc,
           load_sem, z_send, c_send, f_send, t_send, t_recv, s_send, s_recv, o_send, o_recv, m_recv):
    row = lax.axis_index("row")
    col = lax.axis_index("col")
    z, y = row // 2, row % 2
    x, k = col // 2, col % 2
    near = (z // 2 + x) % 2
    far = 1 - near
    core = (z + k) % 2
    half = B // 2
    z_next = z + 1 - 2 * (z % 2)

    def at(z_, y_, x_, k_):
        return (z_ * 2 + y_, x_ * 2 + k_)

    def slot(core_, side, y_, part=None):
        plane = core_ * 2 + side
        sem = (plane * 2 + y_) * 2
        if part is None:
            return m.at[plane, y_], m_recv.at[sem]
        return m.at[plane, y_, pl.ds(part * half, half)], m_recv.at[sem + part]

    def copy(src, dst, send, recv, where):
        return pltpu.make_async_remote_copy(
            src_ref=src, dst_ref=dst, send_sem=send, recv_sem=recv, device_id=where, device_id_type=MESH
        )

    x_mate = at(z, y, 1 - x, k)
    sibling = at(z, y, x, 1 - k)
    y_mate = at(z, 1 - y, x, k)
    z_far = (at(3 - z, y, x, k), at((z + 2) % 4, y, x, k))
    z_near = (at(z_next, y, x, k), at(z_next, 1 - y, x, k))

    barrier = pltpu.get_barrier_semaphore()
    mates = (*z_far, x_mate, y_mate, *z_near, sibling)
    for where in mates:
        pl.semaphore_signal(barrier, inc=1, device_id=where, device_id_type=MESH)

    load_pattern = pltpu.make_async_copy(pattern_ref, pat, load_sem.at[0])
    load_l = pltpu.make_async_copy(l_ref, m.at[core * 2 + near, y], load_sem.at[1])
    load_t = pltpu.make_async_copy(t_ref, t.at[0], load_sem.at[2])
    load_pattern.start()
    load_l.start()
    load_t.start()
    pl.semaphore_wait(barrier, len(mates))

    z_copies = []
    for part in range(2):
        for i, where in enumerate(z_far):
            dst, sem = slot(core, near, y, part)
            z_copies.append(copy(l_ref.at[pl.ds(part * half, half)], dst, z_send.at[part * 2 + i], sem, where))
    mine, mine_sem = slot(core, near, y)
    cross = copy(l_ref, mine, c_send.at[0], mine_sem, y_mate)
    direct = copy(l_ref, mine, c_send.at[1], mine_sem, z_near[0])
    diagonal = copy(l_ref, mine, c_send.at[2], mine_sem, z_near[1])
    t_rows = t.shape[1] // T_CHUNKS
    t_copies = []
    t_forwards = []
    for i in range(T_CHUNKS):
        rows = pl.ds(i * t_rows, t_rows)
        t_copies.append(copy(t_ref.at[rows], t.at[1, rows], t_send.at[i], t_recv.at[i], x_mate))
        t_forwards.append(copy(t.at[1, rows], t.at[3, rows], s_send.at[i], s_recv.at[i], sibling))
    t_sibling = copy(t_ref, t.at[2], o_send.at[0], o_recv.at[0], sibling)

    z_copies[0].start()
    z_copies[1].start()
    t_copies[0].start()
    cross.start()
    z_copies[2].start()
    z_copies[3].start()
    for c in t_copies[1:]:
        c.start()
    direct.start()
    diagonal.start()
    t_sibling.start()

    forwards = []

    def pass_panel(part):
        for i in range(2):
            block, sem = slot((core + 1 + i) % 2, far, y, part)
            f = copy(block, block, f_send.at[part * 2 + i], sem, y_mate)
            f.wait_recv()
            f.start()
            forwards.append(f)

    def pass_inverse(i):
        t_copies[i].wait_recv()
        t_forwards[i].start()

    pass_inverse(0)
    pass_panel(0)
    for i in range(1, T_CHUNKS - 1):
        pass_inverse(i)
    pass_panel(1)
    pass_inverse(T_CHUNKS - 1)

    def arrive(*place):
        block, sem = slot(*place)
        copy(block, block, f_send.at[0], sem, y_mate).wait_recv()

    def product(core_, side, y_):
        plane = core_ * 2 + side
        block_row = (2 * ((side + x) % 2) + (core_ + k) % 2) * 2 + y_
        keep = pat[x, block_row].astype(jnp.float32).astype(jnp.bfloat16)
        columns = pl.ds(pl.multiple_of(y_ * B, B), B)
        return jnp.dot(t[plane, :, columns], m[plane, y_] * keep, preferred_element_type=jnp.float32)

    load_pattern.wait()
    load_l.wait()
    load_t.wait()
    t_sibling.wait_recv()
    arrive(core, near, 1 - y)
    arrive(1 - core, near, y)
    arrive(1 - core, near, 1 - y)
    for f in t_forwards:
        f.wait_recv()
    acc[...] = (product(0, near, 0) + product(0, near, 1) + product(1, near, 0) + product(1, near, 1)
                + product(0, far, y) + product(1, far, y))
    for part in range(2):
        for i in range(2):
            arrive(i, far, 1 - y, part)
    negated = -pat[x, row].astype(jnp.float32)
    out_ref[...] = (acc[...] + product(0, far, 1 - y) + product(1, far, 1 - y)) * negated

    for c in z_copies + [cross, direct, diagonal, t_sibling] + t_copies + t_forwards + forwards:
        c.wait_send()


def fused(trailing_inverse, l_panel, pattern):
    rows, depth = trailing_inverse.shape
    width = l_panel.shape[1]
    dma = pltpu.SemaphoreType.DMA
    operands = [pltpu.with_memory_space_constraint(v, pltpu.HBM) for v in (pattern.T, trailing_inverse, l_panel)]
    return pl.pallas_call(
        kernel,
        out_shape=jax.ShapeDtypeStruct((rows, width), jnp.float32),
        in_specs=[pl.BlockSpec(memory_space=pltpu.HBM)] * 3,
        out_specs=pl.BlockSpec(memory_space=pltpu.VMEM),
        scratch_shapes=[
            pltpu.SMEM(pattern.shape[::-1], jnp.int32),
            pltpu.VMEM((4, rows, depth), jnp.bfloat16),
            pltpu.VMEM((4, 2, B, width), jnp.bfloat16),
            pltpu.VMEM((rows, width), jnp.float32),
            dma((3,)),
            dma((4,)),
            dma((3,)),
            dma((4,)),
            dma((T_CHUNKS,)),
            dma((T_CHUNKS,)),
            dma((T_CHUNKS,)),
            dma((T_CHUNKS,)),
            dma((1,)),
            dma((1,)),
            dma((16,)),
        ],
        compiler_params=pltpu.CompilerParams(
            collective_id=0, has_side_effects=True, vmem_limit_bytes=16 * 1024 * 1024
        ),
        cost_estimate=pl.CostEstimate(
            flops=2 * rows * 4 * depth * width, bytes_accessed=rows * depth * 4, transcendentals=0
        ),
    )(*operands)


def solution(mesh):
    whole_block = (mesh.shape["row"], mesh.shape["col"]) == (8, 4)
    return jax.shard_map(
        fused if whole_block else per_device,
        mesh=mesh,
        in_specs=(P("row", "col"), P("row", "col"), P()),
        out_specs=P("row", "col"),
        check_vma=False,
    )
```

```python
import functools

import jax
import jax.numpy as jnp
from jax import lax
from jax.experimental import pallas as pl
from jax.experimental.pallas import tpu as pltpu
from jax.sharding import PartitionSpec as P

B = 256
RB = 1
MESH = pl.DeviceIdType.MESH
T_CHUNKS = 4


def broadcast(value, axis, source):
    kept = jnp.where(lax.axis_index(axis) == source, value, 0).astype(value.dtype)
    return lax.psum(kept, axis)


def per_device(trailing_inverse, l_panel, pattern):
    grid_row = lax.axis_index("row")
    grid_col = lax.axis_index("col")
    ratio = lax.axis_size("row") // lax.axis_size("col")
    local_rows = l_panel.shape[0]
    supernodes = pattern.shape[1]
    my_pattern = lax.dynamic_slice_in_dim(pattern, grid_row * RB, RB, 0)
    full_row = lax.all_gather(l_panel, "col", axis=1, tiled=True)
    keep = my_pattern.astype(jnp.bfloat16)
    masked_row = (full_row.reshape(RB, B, supernodes, B) * keep[:, None, :, None]).reshape(
        local_rows, supernodes * B
    )
    arrived = []
    columns = []
    for turn in range(ratio):
        root = grid_col * ratio + turn
        piece = broadcast(masked_row, "row", root)
        inverse_cols = lax.dynamic_slice_in_dim(trailing_inverse, turn * local_rows, local_rows, 1)
        arrived.append(piece)
        columns.append(inverse_cols)
    stacked_panel = jnp.concatenate(arrived, 0)
    stacked_inverse = jnp.concatenate(columns, 1)
    partial_value = jnp.dot(stacked_inverse, stacked_panel, preferred_element_type=jnp.float32)
    negated = -my_pattern.astype(jnp.float32)
    signed = (partial_value.reshape(RB, B, supernodes, B) * negated[:, None, :, None]).reshape(
        local_rows, supernodes * B
    )
    return lax.psum_scatter(signed, "col", scatter_dimension=1, tiled=True)


def kernel(pattern_ref, t_ref, l_ref, out_ref, pat, t, m, acc,
           load_sem, z_send, c_send, f_send, t_send, t_recv, s_send, s_recv, o_send, o_recv, m_recv,
           far_sem):
    row = lax.axis_index("row")
    col = lax.axis_index("col")
    z, y = row // 2, row % 2
    x, k = col // 2, col % 2
    near = (z // 2 + x) % 2
    far = 1 - near
    core = (z + k) % 2
    half = B // 2
    z_next = z + 1 - 2 * (z % 2)

    def at(z_, y_, x_, k_):
        return (z_ * 2 + y_, x_ * 2 + k_)

    def slot(core_, side, y_, part=None):
        plane = core_ * 2 + side
        sem = (plane * 2 + y_) * 2
        if part is None:
            return m.at[plane, y_], m_recv.at[sem]
        return m.at[plane, y_, pl.ds(part * half, half)], m_recv.at[sem + part]

    def copy(src, dst, send, recv, where):
        return pltpu.make_async_remote_copy(
            src_ref=src, dst_ref=dst, send_sem=send, recv_sem=recv, device_id=where, device_id_type=MESH
        )

    x_mate = at(z, y, 1 - x, k)
    sibling = at(z, y, x, 1 - k)
    y_mate = at(z, 1 - y, x, k)
    z_far = at((z + 2) % 4, y, x, k)
    z_near = (at(z_next, y, x, k), at(z_next, 1 - y, x, k))
    early = z < 2

    barrier = pltpu.get_barrier_semaphore()
    mates = (y_mate, *z_near, x_mate, sibling)

    def greet(sem, where):
        pl.semaphore_signal(sem, inc=1, device_id=where, device_id_type=MESH)

    @pl.when(early)
    def _():
        greet(barrier, z_far)

    for where in mates:
        greet(barrier, where)

    load_pattern = pltpu.make_async_copy(pattern_ref, pat, load_sem.at[0])
    load_l = pltpu.make_async_copy(l_ref, m.at[core * 2 + near, y], load_sem.at[1])
    load_t = pltpu.make_async_copy(t_ref, t.at[0], load_sem.at[2])
    load_pattern.start()
    load_l.start()
    load_t.start()
    z_copies = []
    for part in range(2):
        dst, sem = slot(core, near, y, part)
        z_copies.append(copy(l_ref.at[pl.ds(part * half, half)], dst, z_send.at[part], sem, z_far))
    mine, mine_sem = slot(core, near, y)
    cross = copy(l_ref, mine, c_send.at[0], mine_sem, y_mate)
    direct = copy(l_ref, mine, c_send.at[1], mine_sem, z_near[0])
    diagonal = copy(l_ref, mine, c_send.at[2], mine_sem, z_near[1])
    t_rows = t.shape[1] // T_CHUNKS
    t_copies = []
    t_forwards = []
    for i in range(T_CHUNKS):
        rows = pl.ds(i * t_rows, t_rows)
        t_copies.append(copy(t_ref.at[rows], t.at[1, rows], t_send.at[i], t_recv.at[i], x_mate))
        t_forwards.append(copy(t.at[1, rows], t.at[3, rows], s_send.at[i], s_recv.at[i], sibling))
    t_sibling = copy(t_ref, t.at[2], o_send.at[0], o_recv.at[0], sibling)

    @pl.when(early)
    def _():
        pl.semaphore_wait(barrier, len(mates))

    @pl.when(jnp.logical_not(early))
    def _():
        pl.semaphore_wait(barrier, len(mates) + 1)
        greet(far_sem, z_far)
        for c in z_copies:
            c.start()

    cross.start()
    t_copies[0].start()
    direct.start()
    diagonal.start()
    for c in t_copies[1:]:
        c.start()
    t_sibling.start()

    @pl.when(early)
    def _():
        pl.semaphore_wait(far_sem, 1)
        for c in z_copies:
            c.start()

    forwards = []

    def pass_panel(part):
        block, sem = slot(core, far, y, part)
        copy(block, block, f_send.at[0], sem, z_far).wait_recv()
        for i, where in enumerate((z_near[1], y_mate, z_near[0])):
            f = copy(block, block, f_send.at[part * 3 + i], sem, where)
            f.start()
            forwards.append(f)

    def pass_inverse(i):
        t_copies[i].wait_recv()
        t_forwards[i].start()

    pass_inverse(0)
    pass_panel(0)
    pass_inverse(1)
    pass_panel(1)
    for i in range(2, T_CHUNKS):
        pass_inverse(i)

    def arrive(*place):
        block, sem = slot(*place)
        copy(block, block, f_send.at[0], sem, y_mate).wait_recv()

    def product(core_, side, y_):
        plane = core_ * 2 + side
        block_row = (2 * ((side + x) % 2) + (core_ + k) % 2) * 2 + y_
        keep = pat[x, block_row].astype(jnp.float32).astype(jnp.bfloat16)
        columns = pl.ds(pl.multiple_of(y_ * B, B), B)
        return jnp.dot(t[plane, :, columns], m[plane, y_] * keep, preferred_element_type=jnp.float32)

    load_pattern.wait()
    load_l.wait()
    load_t.wait()
    t_sibling.wait_recv()
    arrive(core, near, 1 - y)
    arrive(1 - core, near, y)
    arrive(1 - core, near, 1 - y)
    for f in t_forwards:
        f.wait_recv()
    acc[...] = (product(0, near, 0) + product(0, near, 1) + product(1, near, 0) + product(1, near, 1)
                + product(core, far, y))
    for part in range(2):
        arrive(core, far, 1 - y, part)
        arrive(1 - core, far, y, part)
    acc[...] += product(core, far, 1 - y) + product(1 - core, far, y)
    for part in range(2):
        arrive(1 - core, far, 1 - y, part)
    negated = -pat[x, row].astype(jnp.float32)
    out_ref[...] = (acc[...] + product(1 - core, far, 1 - y)) * negated

    for c in z_copies + [cross, direct, diagonal, t_sibling] + t_copies + t_forwards + forwards:
        c.wait_send()


def fused(trailing_inverse, l_panel, pattern):
    rows, depth = trailing_inverse.shape
    width = l_panel.shape[1]
    dma = pltpu.SemaphoreType.DMA
    operands = [pltpu.with_memory_space_constraint(v, pltpu.HBM) for v in (pattern.T, trailing_inverse, l_panel)]
    return pl.pallas_call(
        kernel,
        out_shape=jax.ShapeDtypeStruct((rows, width), jnp.float32),
        in_specs=[pl.BlockSpec(memory_space=pltpu.HBM)] * 3,
        out_specs=pl.BlockSpec(memory_space=pltpu.VMEM),
        scratch_shapes=[
            pltpu.SMEM(pattern.shape[::-1], jnp.int32),
            pltpu.VMEM((4, rows, depth), jnp.bfloat16),
            pltpu.VMEM((4, 2, B, width), jnp.bfloat16),
            pltpu.VMEM((rows, width), jnp.float32),
            dma((3,)),
            dma((2,)),
            dma((3,)),
            dma((6,)),
            dma((T_CHUNKS,)),
            dma((T_CHUNKS,)),
            dma((T_CHUNKS,)),
            dma((T_CHUNKS,)),
            dma((1,)),
            dma((1,)),
            dma((16,)),
            pltpu.SemaphoreType.REGULAR,
        ],
        compiler_params=pltpu.CompilerParams(
            collective_id=0, has_side_effects=True, vmem_limit_bytes=16 * 1024 * 1024
        ),
        cost_estimate=pl.CostEstimate(
            flops=2 * rows * 4 * depth * width, bytes_accessed=rows * depth * 4, transcendentals=0
        ),
    )(*operands)


def solution(mesh):
    whole_block = (mesh.shape["row"], mesh.shape["col"]) == (8, 4)
    return jax.shard_map(
        fused if whole_block else per_device,
        mesh=mesh,
        in_specs=(P("row", "col"), P("row", "col"), P()),
        out_specs=P("row", "col"),
        check_vma=False,
    )
```

```python
import functools

import jax
import jax.numpy as jnp
from jax import lax
from jax.experimental import pallas as pl
from jax.experimental.pallas import tpu as pltpu
from jax.sharding import PartitionSpec as P

B = 256
RB = 1
MESH = pl.DeviceIdType.MESH
T_CHUNKS = 4


def broadcast(value, axis, source):
    kept = jnp.where(lax.axis_index(axis) == source, value, 0).astype(value.dtype)
    return lax.psum(kept, axis)


def per_device(trailing_inverse, l_panel, pattern):
    grid_row = lax.axis_index("row")
    grid_col = lax.axis_index("col")
    ratio = lax.axis_size("row") // lax.axis_size("col")
    local_rows = l_panel.shape[0]
    supernodes = pattern.shape[1]
    my_pattern = lax.dynamic_slice_in_dim(pattern, grid_row * RB, RB, 0)
    full_row = lax.all_gather(l_panel, "col", axis=1, tiled=True)
    keep = my_pattern.astype(jnp.bfloat16)
    masked_row = (full_row.reshape(RB, B, supernodes, B) * keep[:, None, :, None]).reshape(
        local_rows, supernodes * B
    )
    arrived = []
    columns = []
    for turn in range(ratio):
        root = grid_col * ratio + turn
        piece = broadcast(masked_row, "row", root)
        inverse_cols = lax.dynamic_slice_in_dim(trailing_inverse, turn * local_rows, local_rows, 1)
        arrived.append(piece)
        columns.append(inverse_cols)
    stacked_panel = jnp.concatenate(arrived, 0)
    stacked_inverse = jnp.concatenate(columns, 1)
    partial_value = jnp.dot(stacked_inverse, stacked_panel, preferred_element_type=jnp.float32)
    negated = -my_pattern.astype(jnp.float32)
    signed = (partial_value.reshape(RB, B, supernodes, B) * negated[:, None, :, None]).reshape(
        local_rows, supernodes * B
    )
    return lax.psum_scatter(signed, "col", scatter_dimension=1, tiled=True)


def kernel(pattern_ref, t_ref, l_ref, out_ref, pat, t, m, acc,
           load_sem, z_send, c_send, f_send, t_send, t_recv, s_send, s_recv, o_send, o_recv, m_recv,
           ready):
    row = lax.axis_index("row")
    col = lax.axis_index("col")
    z, y = row // 2, row % 2
    x, k = col // 2, col % 2
    near = (z // 2 + x) % 2
    far = 1 - near
    core = (z + k) % 2
    half = B // 2
    z_next = z + 1 - 2 * (z % 2)

    def at(z_, y_, x_, k_):
        return (z_ * 2 + y_, x_ * 2 + k_)

    def slot(core_, side, y_, part=None):
        plane = core_ * 2 + side
        sem = (plane * 2 + y_) * 2
        if part is None:
            return m.at[plane, y_], m_recv.at[sem]
        return m.at[plane, y_, pl.ds(part * half, half)], m_recv.at[sem + part]

    def copy(src, dst, send, recv, where):
        return pltpu.make_async_remote_copy(
            src_ref=src, dst_ref=dst, send_sem=send, recv_sem=recv, device_id=where, device_id_type=MESH
        )

    x_mate = at(z, y, 1 - x, k)
    sibling = at(z, y, x, 1 - k)
    y_mate = at(z, 1 - y, x, k)
    z_far = at((z + 2) % 4, y, x, k)
    z_near = (at(z_next, y, x, k), at(z_next, 1 - y, x, k))

    barrier = pltpu.get_barrier_semaphore()
    mates = (z_far, y_mate, x_mate, z_near[0], z_near[1], sibling)
    is_later = (z < 2, y == 0, x == 0, z % 2 == 0, z % 2 == 0, k == 1)
    n_earlier = z // 2 + y + x + 2 * (z % 2) + 1 - k

    def greet(sem, where):
        pl.semaphore_signal(sem, inc=1, device_id=where, device_id_type=MESH)

    for where, later in zip(mates, is_later):
        @pl.when(later)
        def _(where=where):
            greet(barrier, where)

    load_pattern = pltpu.make_async_copy(pattern_ref, pat, load_sem.at[0])
    load_l = pltpu.make_async_copy(l_ref, m.at[core * 2 + near, y], load_sem.at[1])
    load_t = pltpu.make_async_copy(t_ref, t.at[0], load_sem.at[2])
    load_pattern.start()
    load_l.start()
    load_t.start()
    z_copies = []
    for part in range(2):
        dst, sem = slot(core, near, y, part)
        z_copies.append(copy(l_ref.at[pl.ds(part * half, half)], dst, z_send.at[part], sem, z_far))
    mine, mine_sem = slot(core, near, y)
    cross = copy(l_ref, mine, c_send.at[0], mine_sem, y_mate)
    direct = copy(l_ref, mine, c_send.at[1], mine_sem, z_near[0])
    diagonal = copy(l_ref, mine, c_send.at[2], mine_sem, z_near[1])
    t_rows = t.shape[1] // T_CHUNKS
    t_copies = []
    t_forwards = []
    for i in range(T_CHUNKS):
        rows = pl.ds(i * t_rows, t_rows)
        t_copies.append(copy(t_ref.at[rows], t.at[1, rows], t_send.at[i], t_recv.at[i], x_mate))
        t_forwards.append(copy(t.at[1, rows], t.at[3, rows], s_send.at[i], s_recv.at[i], sibling))
    t_sibling = copy(t_ref, t.at[2], o_send.at[0], o_recv.at[0], sibling)

    @pl.when(n_earlier > 0)
    def _():
        pl.semaphore_wait(barrier, n_earlier)

    groups = (z_copies, [cross], t_copies, [direct], [diagonal], [t_sibling])
    for i, (where, later) in enumerate(zip(mates, is_later)):
        @pl.when(jnp.logical_not(later))
        def _(i=i, where=where):
            greet(ready.at[i], where)
            for c in groups[i]:
                c.start()

    for i in (1, 2, 3, 4, 0, 5):
        @pl.when(is_later[i])
        def _(i=i):
            pl.semaphore_wait(ready.at[i], 1)
            for c in groups[i]:
                c.start()

    forwards = []

    def pass_panel(part):
        block, sem = slot(core, far, y, part)
        copy(block, block, f_send.at[0], sem, z_far).wait_recv()
        for i, where in enumerate((z_near[1], y_mate, z_near[0])):
            f = copy(block, block, f_send.at[part * 3 + i], sem, where)
            f.start()
            forwards.append(f)

    def pass_inverse(i):
        t_copies[i].wait_recv()
        t_forwards[i].start()

    pass_inverse(0)
    pass_panel(0)
    pass_inverse(1)
    pass_panel(1)
    for i in range(2, T_CHUNKS):
        pass_inverse(i)

    def arrive(*place):
        block, sem = slot(*place)
        copy(block, block, f_send.at[0], sem, y_mate).wait_recv()

    def product(core_, side, y_):
        plane = core_ * 2 + side
        block_row = (2 * ((side + x) % 2) + (core_ + k) % 2) * 2 + y_
        keep = pat[x, block_row].astype(jnp.float32).astype(jnp.bfloat16)
        columns = pl.ds(pl.multiple_of(y_ * B, B), B)
        return jnp.dot(t[plane, :, columns], m[plane, y_] * keep, preferred_element_type=jnp.float32)

    load_pattern.wait()
    load_l.wait()
    load_t.wait()
    t_sibling.wait_recv()
    arrive(core, near, 1 - y)
    arrive(1 - core, near, y)
    arrive(1 - core, near, 1 - y)
    for f in t_forwards:
        f.wait_recv()
    acc[...] = (product(0, near, 0) + product(0, near, 1) + product(1, near, 0) + product(1, near, 1)
                + product(core, far, y))
    for part in range(2):
        arrive(core, far, 1 - y, part)
        arrive(1 - core, far, y, part)
    acc[...] += product(core, far, 1 - y) + product(1 - core, far, y)
    for part in range(2):
        arrive(1 - core, far, 1 - y, part)
    negated = -pat[x, row].astype(jnp.float32)
    out_ref[...] = (acc[...] + product(1 - core, far, 1 - y)) * negated

    for c in z_copies + [cross, direct, diagonal, t_sibling] + t_copies + t_forwards + forwards:
        c.wait_send()


def fused(trailing_inverse, l_panel, pattern):
    rows, depth = trailing_inverse.shape
    width = l_panel.shape[1]
    dma = pltpu.SemaphoreType.DMA
    operands = [pltpu.with_memory_space_constraint(v, pltpu.HBM) for v in (pattern.T, trailing_inverse, l_panel)]
    return pl.pallas_call(
        kernel,
        out_shape=jax.ShapeDtypeStruct((rows, width), jnp.float32),
        in_specs=[pl.BlockSpec(memory_space=pltpu.HBM)] * 3,
        out_specs=pl.BlockSpec(memory_space=pltpu.VMEM),
        scratch_shapes=[
            pltpu.SMEM(pattern.shape[::-1], jnp.int32),
            pltpu.VMEM((4, rows, depth), jnp.bfloat16),
            pltpu.VMEM((4, 2, B, width), jnp.bfloat16),
            pltpu.VMEM((rows, width), jnp.float32),
            dma((3,)),
            dma((2,)),
            dma((3,)),
            dma((6,)),
            dma((T_CHUNKS,)),
            dma((T_CHUNKS,)),
            dma((T_CHUNKS,)),
            dma((T_CHUNKS,)),
            dma((1,)),
            dma((1,)),
            dma((16,)),
            pltpu.SemaphoreType.REGULAR((6,)),
        ],
        compiler_params=pltpu.CompilerParams(
            collective_id=0, has_side_effects=True, vmem_limit_bytes=16 * 1024 * 1024
        ),
        cost_estimate=pl.CostEstimate(
            flops=2 * rows * 4 * depth * width, bytes_accessed=rows * depth * 4, transcendentals=0
        ),
    )(*operands)


def solution(mesh):
    whole_block = (mesh.shape["row"], mesh.shape["col"]) == (8, 4)
    return jax.shard_map(
        fused if whole_block else per_device,
        mesh=mesh,
        in_specs=(P("row", "col"), P("row", "col"), P()),
        out_specs=P("row", "col"),
        check_vma=False,
    )
```

```python
import functools

import jax
import jax.numpy as jnp
from jax import lax
from jax.experimental import pallas as pl
from jax.experimental.pallas import tpu as pltpu
from jax.sharding import PartitionSpec as P

B = 256
RB = 1
MESH = pl.DeviceIdType.MESH
T_CHUNKS = 4


def broadcast(value, axis, source):
    kept = jnp.where(lax.axis_index(axis) == source, value, 0).astype(value.dtype)
    return lax.psum(kept, axis)


def per_device(trailing_inverse, l_panel, pattern):
    grid_row = lax.axis_index("row")
    grid_col = lax.axis_index("col")
    ratio = lax.axis_size("row") // lax.axis_size("col")
    local_rows = l_panel.shape[0]
    supernodes = pattern.shape[1]
    my_pattern = lax.dynamic_slice_in_dim(pattern, grid_row * RB, RB, 0)
    full_row = lax.all_gather(l_panel, "col", axis=1, tiled=True)
    keep = my_pattern.astype(jnp.bfloat16)
    masked_row = (full_row.reshape(RB, B, supernodes, B) * keep[:, None, :, None]).reshape(
        local_rows, supernodes * B
    )
    arrived = []
    columns = []
    for turn in range(ratio):
        root = grid_col * ratio + turn
        piece = broadcast(masked_row, "row", root)
        inverse_cols = lax.dynamic_slice_in_dim(trailing_inverse, turn * local_rows, local_rows, 1)
        arrived.append(piece)
        columns.append(inverse_cols)
    stacked_panel = jnp.concatenate(arrived, 0)
    stacked_inverse = jnp.concatenate(columns, 1)
    partial_value = jnp.dot(stacked_inverse, stacked_panel, preferred_element_type=jnp.float32)
    negated = -my_pattern.astype(jnp.float32)
    signed = (partial_value.reshape(RB, B, supernodes, B) * negated[:, None, :, None]).reshape(
        local_rows, supernodes * B
    )
    return lax.psum_scatter(signed, "col", scatter_dimension=1, tiled=True)


def kernel(pattern_ref, t_ref, l_ref, out_ref, pat, t, m, acc,
           load_sem, z_send, c_send, f_send, t_send, t_recv, s_send, s_recv, o_send, o_recv, m_recv,
           ready):
    row = lax.axis_index("row")
    col = lax.axis_index("col")
    z, y = row // 2, row % 2
    x, k = col // 2, col % 2
    near = (z // 2 + x) % 2
    far = 1 - near
    core = (z + k) % 2
    half = B // 2
    z_next = z + 1 - 2 * (z % 2)

    def at(z_, y_, x_, k_):
        return (z_ * 2 + y_, x_ * 2 + k_)

    def slot(core_, side, y_, part=None):
        plane = core_ * 2 + side
        sem = (plane * 2 + y_) * 2
        if part is None:
            return m.at[plane, y_], m_recv.at[sem]
        return m.at[plane, y_, pl.ds(part * half, half)], m_recv.at[sem + part]

    def copy(src, dst, send, recv, where):
        return pltpu.make_async_remote_copy(
            src_ref=src, dst_ref=dst, send_sem=send, recv_sem=recv, device_id=where, device_id_type=MESH
        )

    x_mate = at(z, y, 1 - x, k)
    sibling = at(z, y, x, 1 - k)
    y_mate = at(z, 1 - y, x, k)
    z_far = at((z + 2) % 4, y, x, k)
    z_near = (at(z_next, y, x, k), at(z_next, 1 - y, x, k))

    barrier = pltpu.get_barrier_semaphore()
    mates = (z_far, y_mate, x_mate, z_near[0], z_near[1], sibling)
    is_later = (z < 2, y == 0, x == 0, z % 2 == 0, z % 2 == 0, k == 1)
    n_earlier = z // 2 + y + x + 2 * (z % 2) + 1 - k

    def greet(sem, where):
        pl.semaphore_signal(sem, inc=1, device_id=where, device_id_type=MESH)

    for where, later in zip(mates, is_later):
        @pl.when(later)
        def _(where=where):
            greet(barrier, where)

    load_pattern = pltpu.make_async_copy(pattern_ref, pat, load_sem.at[0])
    load_l = pltpu.make_async_copy(l_ref, m.at[core * 2 + near, y], load_sem.at[1])
    load_t = pltpu.make_async_copy(t_ref, t.at[0], load_sem.at[2])
    load_pattern.start()
    load_l.start()
    load_t.start()
    z_copies = []
    for part in range(2):
        dst, sem = slot(core, near, y, part)
        z_copies.append(copy(l_ref.at[pl.ds(part * half, half)], dst, z_send.at[part], sem, z_far))
    mine, mine_sem = slot(core, near, y)
    cross = copy(l_ref, mine, c_send.at[0], mine_sem, y_mate)
    direct = copy(l_ref, mine, c_send.at[1], mine_sem, z_near[0])
    diagonal = copy(l_ref, mine, c_send.at[2], mine_sem, z_near[1])
    t_rows = t.shape[1] // T_CHUNKS
    t_copies = []
    t_forwards = []
    for i in range(T_CHUNKS):
        rows = pl.ds(i * t_rows, t_rows)
        t_copies.append(copy(t_ref.at[rows], t.at[1, rows], t_send.at[i], t_recv.at[i], x_mate))
        t_forwards.append(copy(t.at[1, rows], t.at[3, rows], s_send.at[i], s_recv.at[i], sibling))
    t_sibling = copy(t_ref, t.at[2], o_send.at[0], o_recv.at[0], sibling)

    @pl.when(n_earlier > 0)
    def _():
        pl.semaphore_wait(barrier, n_earlier)

    groups = (z_copies, [cross], t_copies, [direct], [diagonal], [t_sibling])
    for i, (where, later) in enumerate(zip(mates, is_later)):
        @pl.when(jnp.logical_not(later))
        def _(i=i, where=where):
            greet(ready.at[i], where)
            for c in groups[i]:
                c.start()

    for i in (1, 2, 3, 4, 0, 5):
        @pl.when(is_later[i])
        def _(i=i):
            pl.semaphore_wait(ready.at[i], 1)
            for c in groups[i]:
                c.start()

    forwards = []

    def pass_panel(part):
        block, sem = slot(core, far, y, part)
        copy(block, block, f_send.at[0], sem, z_far).wait_recv()
        for i, where in enumerate((z_near[1], y_mate, z_near[0])):
            f = copy(block, block, f_send.at[part * 3 + i], sem, where)
            f.start()
            forwards.append(f)

    def pass_inverse(i):
        t_copies[i].wait_recv()
        t_forwards[i].start()

    pass_panel(0)
    pass_panel(1)

    def arrive(*place):
        block, sem = slot(*place)
        copy(block, block, f_send.at[0], sem, y_mate).wait_recv()

    def product(core_, side, y_):
        plane = core_ * 2 + side
        block_row = (2 * ((side + x) % 2) + (core_ + k) % 2) * 2 + y_
        keep = pat[x, block_row].astype(jnp.float32).astype(jnp.bfloat16)
        columns = pl.ds(pl.multiple_of(y_ * B, B), B)
        return jnp.dot(t[plane, :, columns], m[plane, y_] * keep, preferred_element_type=jnp.float32)

    def near_product(side):
        return product(0, side, 0) + product(0, side, 1) + product(1, side, 0) + product(1, side, 1)

    load_pattern.wait()
    load_l.wait()
    load_t.wait()
    arrive(core, near, 1 - y)
    arrive(1 - core, near, y)
    arrive(1 - core, near, 1 - y)
    t_sibling.wait_recv()

    @pl.when(near == 0)
    def _():
        acc[...] = near_product(0)

    for i in range(T_CHUNKS):
        pass_inverse(i)
    for f in t_forwards:
        f.wait_recv()

    @pl.when(near == 1)
    def _():
        acc[...] = near_product(1)

    acc[...] += product(core, far, y)
    for part in range(2):
        arrive(core, far, 1 - y, part)
        arrive(1 - core, far, y, part)
    acc[...] += product(core, far, 1 - y) + product(1 - core, far, y)
    for part in range(2):
        arrive(1 - core, far, 1 - y, part)
    negated = -pat[x, row].astype(jnp.float32)
    out_ref[...] = (acc[...] + product(1 - core, far, 1 - y)) * negated

    for c in z_copies + [cross, direct, diagonal, t_sibling] + t_copies + t_forwards + forwards:
        c.wait_send()


def fused(trailing_inverse, l_panel, pattern):
    rows, depth = trailing_inverse.shape
    width = l_panel.shape[1]
    dma = pltpu.SemaphoreType.DMA
    operands = [pltpu.with_memory_space_constraint(v, pltpu.HBM) for v in (pattern.T, trailing_inverse, l_panel)]
    return pl.pallas_call(
        kernel,
        out_shape=jax.ShapeDtypeStruct((rows, width), jnp.float32),
        in_specs=[pl.BlockSpec(memory_space=pltpu.HBM)] * 3,
        out_specs=pl.BlockSpec(memory_space=pltpu.VMEM),
        scratch_shapes=[
            pltpu.SMEM(pattern.shape[::-1], jnp.int32),
            pltpu.VMEM((4, rows, depth), jnp.bfloat16),
            pltpu.VMEM((4, 2, B, width), jnp.bfloat16),
            pltpu.VMEM((rows, width), jnp.float32),
            dma((3,)),
            dma((2,)),
            dma((3,)),
            dma((6,)),
            dma((T_CHUNKS,)),
            dma((T_CHUNKS,)),
            dma((T_CHUNKS,)),
            dma((T_CHUNKS,)),
            dma((1,)),
            dma((1,)),
            dma((16,)),
            pltpu.SemaphoreType.REGULAR((6,)),
        ],
        compiler_params=pltpu.CompilerParams(
            collective_id=0, has_side_effects=True, vmem_limit_bytes=16 * 1024 * 1024
        ),
        cost_estimate=pl.CostEstimate(
            flops=2 * rows * 4 * depth * width, bytes_accessed=rows * depth * 4, transcendentals=0
        ),
    )(*operands)


def solution(mesh):
    whole_block = (mesh.shape["row"], mesh.shape["col"]) == (8, 4)
    return jax.shard_map(
        fused if whole_block else per_device,
        mesh=mesh,
        in_specs=(P("row", "col"), P("row", "col"), P()),
        out_specs=P("row", "col"),
        check_vma=False,
    )
```

```python
import functools

import jax
import jax.numpy as jnp
from jax import lax
from jax.experimental import pallas as pl
from jax.experimental.pallas import tpu as pltpu
from jax.sharding import PartitionSpec as P

B = 256
RB = 1
MESH = pl.DeviceIdType.MESH
T_CHUNKS = 4


def broadcast(value, axis, source):
    kept = jnp.where(lax.axis_index(axis) == source, value, 0).astype(value.dtype)
    return lax.psum(kept, axis)


def per_device(trailing_inverse, l_panel, pattern):
    grid_row = lax.axis_index("row")
    grid_col = lax.axis_index("col")
    ratio = lax.axis_size("row") // lax.axis_size("col")
    local_rows = l_panel.shape[0]
    supernodes = pattern.shape[1]
    my_pattern = lax.dynamic_slice_in_dim(pattern, grid_row * RB, RB, 0)
    full_row = lax.all_gather(l_panel, "col", axis=1, tiled=True)
    keep = my_pattern.astype(jnp.bfloat16)
    masked_row = (full_row.reshape(RB, B, supernodes, B) * keep[:, None, :, None]).reshape(
        local_rows, supernodes * B
    )
    arrived = []
    columns = []
    for turn in range(ratio):
        root = grid_col * ratio + turn
        piece = broadcast(masked_row, "row", root)
        inverse_cols = lax.dynamic_slice_in_dim(trailing_inverse, turn * local_rows, local_rows, 1)
        arrived.append(piece)
        columns.append(inverse_cols)
    stacked_panel = jnp.concatenate(arrived, 0)
    stacked_inverse = jnp.concatenate(columns, 1)
    partial_value = jnp.dot(stacked_inverse, stacked_panel, preferred_element_type=jnp.float32)
    negated = -my_pattern.astype(jnp.float32)
    signed = (partial_value.reshape(RB, B, supernodes, B) * negated[:, None, :, None]).reshape(
        local_rows, supernodes * B
    )
    return lax.psum_scatter(signed, "col", scatter_dimension=1, tiled=True)


def kernel(pattern_ref, t_ref, l_ref, out_ref, pat, t, m, acc,
           load_sem, z_send, c_send, f_send, t_send, t_recv, s_send, s_recv, o_send, o_recv, m_recv,
           ready):
    row = lax.axis_index("row")
    col = lax.axis_index("col")
    z, y = row // 2, row % 2
    x, k = col // 2, col % 2
    near = (z // 2 + x) % 2
    far = 1 - near
    core = (z + k) % 2
    half = B // 2
    z_next = z + 1 - 2 * (z % 2)

    def at(z_, y_, x_, k_):
        return (z_ * 2 + y_, x_ * 2 + k_)

    def slot(core_, side, y_, part=None):
        plane = core_ * 2 + side
        sem = (plane * 2 + y_) * 2
        if part is None:
            return m.at[plane, y_], m_recv.at[sem]
        return m.at[plane, y_, pl.ds(part * half, half)], m_recv.at[sem + part]

    def copy(src, dst, send, recv, where):
        return pltpu.make_async_remote_copy(
            src_ref=src, dst_ref=dst, send_sem=send, recv_sem=recv, device_id=where, device_id_type=MESH
        )

    x_mate = at(z, y, 1 - x, k)
    sibling = at(z, y, x, 1 - k)
    y_mate = at(z, 1 - y, x, k)
    z_far = at((z + 2) % 4, y, x, k)
    z_near = at(z_next, y, x, k)

    barrier = pltpu.get_barrier_semaphore()
    mates = (z_far, y_mate, x_mate, z_near, sibling)
    is_later = (z < 2, y == 0, x == 0, z % 2 == 0, k == 1)
    n_earlier = z // 2 + y + x + z % 2 + 1 - k

    def greet(sem, where):
        pl.semaphore_signal(sem, inc=1, device_id=where, device_id_type=MESH)

    for where, later in zip(mates, is_later):
        @pl.when(later)
        def _(where=where):
            greet(barrier, where)

    load_pattern = pltpu.make_async_copy(pattern_ref, pat, load_sem.at[0])
    load_l = pltpu.make_async_copy(l_ref, m.at[core * 2 + near, y], load_sem.at[1])
    load_t = pltpu.make_async_copy(t_ref, t.at[0], load_sem.at[2])
    load_pattern.start()
    load_l.start()
    load_t.start()
    z_copies = []
    for part in range(2):
        dst, sem = slot(core, near, y, part)
        z_copies.append(copy(l_ref.at[pl.ds(part * half, half)], dst, z_send.at[part], sem, z_far))
    mine, mine_sem = slot(core, near, y)
    cross = copy(l_ref, mine, c_send.at[0], mine_sem, y_mate)
    direct = copy(l_ref, mine, c_send.at[1], mine_sem, z_near)
    t_rows = t.shape[1] // T_CHUNKS
    t_copies = []
    t_forwards = []
    for i in range(T_CHUNKS):
        rows = pl.ds(i * t_rows, t_rows)
        t_copies.append(copy(t_ref.at[rows], t.at[1, rows], t_send.at[i], t_recv.at[i], x_mate))
        t_forwards.append(copy(t.at[1, rows], t.at[3, rows], s_send.at[i], s_recv.at[i], sibling))
    t_sibling = copy(t_ref, t.at[2], o_send.at[0], o_recv.at[0], sibling)

    @pl.when(n_earlier > 0)
    def _():
        pl.semaphore_wait(barrier, n_earlier)

    groups = (z_copies, [cross], t_copies, [direct], [t_sibling])
    for i, (where, later) in enumerate(zip(mates, is_later)):
        @pl.when(jnp.logical_not(later))
        def _(i=i, where=where):
            greet(ready.at[i], where)
            for c in groups[i]:
                c.start()

    for i in (1, 2, 3, 0, 4):
        @pl.when(is_later[i])
        def _(i=i):
            pl.semaphore_wait(ready.at[i], 1)
            for c in groups[i]:
                c.start()

    forwards = []

    def pass_on(place, *targets):
        block, sem = slot(*place)
        copy(block, block, f_send.at[0], sem, y_mate).wait_recv()
        for where in targets:
            f = copy(block, block, f_send.at[len(forwards)], sem, where)
            f.start()
            forwards.append(f)

    def pass_inverse(i):
        t_copies[i].wait_recv()
        t_forwards[i].start()

    def arrive(*place):
        block, sem = slot(*place)
        copy(block, block, f_send.at[0], sem, y_mate).wait_recv()

    def product(core_, side, y_):
        plane = core_ * 2 + side
        block_row = (2 * ((side + x) % 2) + (core_ + k) % 2) * 2 + y_
        keep = pat[x, block_row].astype(jnp.float32).astype(jnp.bfloat16)
        columns = pl.ds(pl.multiple_of(y_ * B, B), B)
        return jnp.dot(t[plane, :, columns], m[plane, y_] * keep, preferred_element_type=jnp.float32)

    def near_product(side):
        return product(0, side, 0) + product(0, side, 1) + product(1, side, 0) + product(1, side, 1)

    pass_on((1 - core, near, y), y_mate)
    for part in range(2):
        pass_on((core, far, y, part), z_near, y_mate)

    load_pattern.wait()
    load_l.wait()
    load_t.wait()
    arrive(core, near, 1 - y)
    arrive(1 - core, near, 1 - y)
    t_sibling.wait_recv()

    @pl.when(near == 0)
    def _():
        acc[...] = near_product(0)

    pass_on((1 - core, far, y, 0), y_mate)
    pass_inverse(0)
    pass_inverse(1)
    pass_on((1 - core, far, y, 1), y_mate)
    for i in range(2, T_CHUNKS):
        pass_inverse(i)
    for f in t_forwards:
        f.wait_recv()

    @pl.when(near == 1)
    def _():
        acc[...] = near_product(1)

    acc[...] += product(core, far, y) + product(1 - core, far, y)
    for part in range(2):
        arrive(core, far, 1 - y, part)
    acc[...] += product(core, far, 1 - y)
    for part in range(2):
        arrive(1 - core, far, 1 - y, part)
    negated = -pat[x, row].astype(jnp.float32)
    out_ref[...] = (acc[...] + product(1 - core, far, 1 - y)) * negated

    for c in z_copies + [cross, direct, t_sibling] + t_copies + t_forwards + forwards:
        c.wait_send()


def fused(trailing_inverse, l_panel, pattern):
    rows, depth = trailing_inverse.shape
    width = l_panel.shape[1]
    dma = pltpu.SemaphoreType.DMA
    operands = [pltpu.with_memory_space_constraint(v, pltpu.HBM) for v in (pattern.T, trailing_inverse, l_panel)]
    return pl.pallas_call(
        kernel,
        out_shape=jax.ShapeDtypeStruct((rows, width), jnp.float32),
        in_specs=[pl.BlockSpec(memory_space=pltpu.HBM)] * 3,
        out_specs=pl.BlockSpec(memory_space=pltpu.VMEM),
        scratch_shapes=[
            pltpu.SMEM(pattern.shape[::-1], jnp.int32),
            pltpu.VMEM((4, rows, depth), jnp.bfloat16),
            pltpu.VMEM((4, 2, B, width), jnp.bfloat16),
            pltpu.VMEM((rows, width), jnp.float32),
            dma((3,)),
            dma((2,)),
            dma((2,)),
            dma((7,)),
            dma((T_CHUNKS,)),
            dma((T_CHUNKS,)),
            dma((T_CHUNKS,)),
            dma((T_CHUNKS,)),
            dma((1,)),
            dma((1,)),
            dma((16,)),
            pltpu.SemaphoreType.REGULAR((5,)),
        ],
        compiler_params=pltpu.CompilerParams(
            collective_id=0, has_side_effects=True, vmem_limit_bytes=16 * 1024 * 1024
        ),
        cost_estimate=pl.CostEstimate(
            flops=2 * rows * 4 * depth * width, bytes_accessed=rows * depth * 4, transcendentals=0
        ),
    )(*operands)


def solution(mesh):
    whole_block = (mesh.shape["row"], mesh.shape["col"]) == (8, 4)
    return jax.shard_map(
        fused if whole_block else per_device,
        mesh=mesh,
        in_specs=(P("row", "col"), P("row", "col"), P()),
        out_specs=P("row", "col"),
        check_vma=False,
    )
```

```python
import functools

import jax
import jax.numpy as jnp
from jax import lax
from jax.experimental import pallas as pl
from jax.experimental.pallas import tpu as pltpu
from jax.sharding import PartitionSpec as P

B = 256
RB = 1
MESH = pl.DeviceIdType.MESH
T_CHUNKS = 4


def broadcast(value, axis, source):
    kept = jnp.where(lax.axis_index(axis) == source, value, 0).astype(value.dtype)
    return lax.psum(kept, axis)


def per_device(trailing_inverse, l_panel, pattern):
    grid_row = lax.axis_index("row")
    grid_col = lax.axis_index("col")
    ratio = lax.axis_size("row") // lax.axis_size("col")
    local_rows = l_panel.shape[0]
    supernodes = pattern.shape[1]
    my_pattern = lax.dynamic_slice_in_dim(pattern, grid_row * RB, RB, 0)
    full_row = lax.all_gather(l_panel, "col", axis=1, tiled=True)
    keep = my_pattern.astype(jnp.bfloat16)
    masked_row = (full_row.reshape(RB, B, supernodes, B) * keep[:, None, :, None]).reshape(
        local_rows, supernodes * B
    )
    arrived = []
    columns = []
    for turn in range(ratio):
        root = grid_col * ratio + turn
        piece = broadcast(masked_row, "row", root)
        inverse_cols = lax.dynamic_slice_in_dim(trailing_inverse, turn * local_rows, local_rows, 1)
        arrived.append(piece)
        columns.append(inverse_cols)
    stacked_panel = jnp.concatenate(arrived, 0)
    stacked_inverse = jnp.concatenate(columns, 1)
    partial_value = jnp.dot(stacked_inverse, stacked_panel, preferred_element_type=jnp.float32)
    negated = -my_pattern.astype(jnp.float32)
    signed = (partial_value.reshape(RB, B, supernodes, B) * negated[:, None, :, None]).reshape(
        local_rows, supernodes * B
    )
    return lax.psum_scatter(signed, "col", scatter_dimension=1, tiled=True)


def kernel(pattern_ref, t_ref, l_ref, out_ref, pat, t, m, acc,
           load_sem, z_send, c_send, f_send, t_send, t_recv, s_send, s_recv, o_send, o_recv, m_recv,
           ready):
    row = lax.axis_index("row")
    col = lax.axis_index("col")
    z, y = row // 2, row % 2
    x, k = col // 2, col % 2
    near = (z // 2 + x) % 2
    far = 1 - near
    core = (z + k) % 2
    half = B // 2
    z_next = z + 1 - 2 * (z % 2)

    def at(z_, y_, x_, k_):
        return (z_ * 2 + y_, x_ * 2 + k_)

    def slot(core_, side, y_, part=None):
        plane = core_ * 2 + side
        sem = (plane * 2 + y_) * 2
        if part is None:
            return m.at[plane, y_], m_recv.at[sem]
        return m.at[plane, y_, pl.ds(part * half, half)], m_recv.at[sem + part]

    def copy(src, dst, send, recv, where):
        return pltpu.make_async_remote_copy(
            src_ref=src, dst_ref=dst, send_sem=send, recv_sem=recv, device_id=where, device_id_type=MESH
        )

    x_mate = at(z, y, 1 - x, k)
    sibling = at(z, y, x, 1 - k)
    y_mate = at(z, 1 - y, x, k)
    z_far = at((z + 2) % 4, y, x, k)
    z_near = (at(z_next, y, x, k), at(z_next, 1 - y, x, k))

    barrier = pltpu.get_barrier_semaphore()
    mates = (z_far, y_mate, z_near[0], z_near[1], x_mate, sibling)
    is_later = (z < 2, y == 0, z % 2 == 0, z % 2 == 0, x == 0, k == 1)
    n_earlier = z // 2 + y + x + 2 * (z % 2) + 1 - k

    def greet(sem, where):
        pl.semaphore_signal(sem, inc=1, device_id=where, device_id_type=MESH)

    for where, later in zip(mates, is_later):
        @pl.when(later)
        def _(where=where):
            greet(barrier, where)

    load_pattern = pltpu.make_async_copy(pattern_ref, pat, load_sem.at[0])
    load_l = pltpu.make_async_copy(l_ref, m.at[core * 2 + near, y], load_sem.at[1])
    load_t = pltpu.make_async_copy(t_ref, t.at[0], load_sem.at[2])
    load_pattern.start()
    load_l.start()
    load_t.start()
    z_copies = []
    for part in range(2):
        dst, sem = slot(core, near, y, part)
        z_copies.append(copy(l_ref.at[pl.ds(part * half, half)], dst, z_send.at[part], sem, z_far))
    mine, mine_sem = slot(core, near, y)
    cross = copy(l_ref, mine, c_send.at[0], mine_sem, y_mate)
    direct = copy(l_ref, mine, c_send.at[1], mine_sem, z_near[0])
    diagonal = copy(l_ref, mine, c_send.at[2], mine_sem, z_near[1])
    t_rows = t.shape[1] // T_CHUNKS
    t_copies = []
    t_forwards = []
    for i in range(T_CHUNKS):
        rows = pl.ds(i * t_rows, t_rows)
        t_copies.append(copy(t_ref.at[rows], t.at[1, rows], t_send.at[i], t_recv.at[i], x_mate))
        t_forwards.append(copy(t.at[1, rows], t.at[3, rows], s_send.at[i], s_recv.at[i], sibling))
    t_sibling = copy(t_ref, t.at[2], o_send.at[0], o_recv.at[0], sibling)

    @pl.when(n_earlier > 0)
    def _():
        pl.semaphore_wait(barrier, n_earlier)

    groups = (z_copies, [cross], [direct], [diagonal], t_copies, [t_sibling])
    for i, (where, later) in enumerate(zip(mates, is_later)):
        @pl.when(jnp.logical_not(later))
        def _(i=i, where=where):
            greet(ready.at[i], where)
            for c in groups[i]:
                c.start()

    for i in (1, 2, 3, 4, 0, 5):
        @pl.when(is_later[i])
        def _(i=i):
            pl.semaphore_wait(ready.at[i], 1)
            for c in groups[i]:
                c.start()

    forwards = []

    def pass_panel(part):
        block, sem = slot(core, far, y, part)
        copy(block, block, f_send.at[0], sem, z_far).wait_recv()
        for i, where in enumerate((z_near[1], y_mate, z_near[0])):
            f = copy(block, block, f_send.at[part * 3 + i], sem, where)
            f.start()
            forwards.append(f)

    def pass_inverse(i):
        t_copies[i].wait_recv()
        t_forwards[i].start()

    pass_panel(0)
    pass_panel(1)

    def arrive(*place):
        block, sem = slot(*place)
        copy(block, block, f_send.at[0], sem, y_mate).wait_recv()

    def product(core_, side, y_):
        plane = core_ * 2 + side
        block_row = (2 * ((side + x) % 2) + (core_ + k) % 2) * 2 + y_
        keep = pat[x, block_row].astype(jnp.float32).astype(jnp.bfloat16)
        columns = pl.ds(pl.multiple_of(y_ * B, B), B)
        return jnp.dot(t[plane, :, columns], m[plane, y_] * keep, preferred_element_type=jnp.float32)

    def near_product(side):
        return product(0, side, 0) + product(0, side, 1) + product(1, side, 0) + product(1, side, 1)

    load_pattern.wait()
    load_l.wait()
    load_t.wait()
    arrive(core, near, 1 - y)
    arrive(1 - core, near, y)
    arrive(1 - core, near, 1 - y)
    t_sibling.wait_recv()

    @pl.when(near == 0)
    def _():
        acc[...] = near_product(0)

    for i in range(T_CHUNKS):
        pass_inverse(i)
    for f in t_forwards:
        f.wait_recv()

    @pl.when(near == 1)
    def _():
        acc[...] = near_product(1)

    acc[...] += product(core, far, y)
    for part in range(2):
        arrive(core, far, 1 - y, part)
        arrive(1 - core, far, y, part)
    acc[...] += product(core, far, 1 - y) + product(1 - core, far, y)
    for part in range(2):
        arrive(1 - core, far, 1 - y, part)
    negated = -pat[x, row].astype(jnp.float32)
    out_ref[...] = (acc[...] + product(1 - core, far, 1 - y)) * negated

    for c in z_copies + [cross, direct, diagonal, t_sibling] + t_copies + t_forwards + forwards:
        c.wait_send()


def fused(trailing_inverse, l_panel, pattern):
    rows, depth = trailing_inverse.shape
    width = l_panel.shape[1]
    dma = pltpu.SemaphoreType.DMA
    operands = [pltpu.with_memory_space_constraint(v, pltpu.HBM) for v in (pattern.T, trailing_inverse, l_panel)]
    return pl.pallas_call(
        kernel,
        out_shape=jax.ShapeDtypeStruct((rows, width), jnp.float32),
        in_specs=[pl.BlockSpec(memory_space=pltpu.HBM)] * 3,
        out_specs=pl.BlockSpec(memory_space=pltpu.VMEM),
        scratch_shapes=[
            pltpu.SMEM(pattern.shape[::-1], jnp.int32),
            pltpu.VMEM((4, rows, depth), jnp.bfloat16),
            pltpu.VMEM((4, 2, B, width), jnp.bfloat16),
            pltpu.VMEM((rows, width), jnp.float32),
            dma((3,)),
            dma((2,)),
            dma((3,)),
            dma((6,)),
            dma((T_CHUNKS,)),
            dma((T_CHUNKS,)),
            dma((T_CHUNKS,)),
            dma((T_CHUNKS,)),
            dma((1,)),
            dma((1,)),
            dma((16,)),
            pltpu.SemaphoreType.REGULAR((6,)),
        ],
        compiler_params=pltpu.CompilerParams(
            collective_id=0, has_side_effects=True, vmem_limit_bytes=16 * 1024 * 1024
        ),
        cost_estimate=pl.CostEstimate(
            flops=2 * rows * 4 * depth * width, bytes_accessed=rows * depth * 4, transcendentals=0
        ),
    )(*operands)


def solution(mesh):
    whole_block = (mesh.shape["row"], mesh.shape["col"]) == (8, 4)
    return jax.shard_map(
        fused if whole_block else per_device,
        mesh=mesh,
        in_specs=(P("row", "col"), P("row", "col"), P()),
        out_specs=P("row", "col"),
        check_vma=False,
    )
```

```python
import functools

import jax
import jax.numpy as jnp
from jax import lax
from jax.experimental import pallas as pl
from jax.experimental.pallas import tpu as pltpu
from jax.sharding import PartitionSpec as P

B = 256
RB = 1
MESH = pl.DeviceIdType.MESH
T_CHUNKS = 4


def broadcast(value, axis, source):
    kept = jnp.where(lax.axis_index(axis) == source, value, 0).astype(value.dtype)
    return lax.psum(kept, axis)


def per_device(trailing_inverse, l_panel, pattern):
    grid_row = lax.axis_index("row")
    grid_col = lax.axis_index("col")
    ratio = lax.axis_size("row") // lax.axis_size("col")
    local_rows = l_panel.shape[0]
    supernodes = pattern.shape[1]
    my_pattern = lax.dynamic_slice_in_dim(pattern, grid_row * RB, RB, 0)
    full_row = lax.all_gather(l_panel, "col", axis=1, tiled=True)
    keep = my_pattern.astype(jnp.bfloat16)
    masked_row = (full_row.reshape(RB, B, supernodes, B) * keep[:, None, :, None]).reshape(
        local_rows, supernodes * B
    )
    arrived = []
    columns = []
    for turn in range(ratio):
        root = grid_col * ratio + turn
        piece = broadcast(masked_row, "row", root)
        inverse_cols = lax.dynamic_slice_in_dim(trailing_inverse, turn * local_rows, local_rows, 1)
        arrived.append(piece)
        columns.append(inverse_cols)
    stacked_panel = jnp.concatenate(arrived, 0)
    stacked_inverse = jnp.concatenate(columns, 1)
    partial_value = jnp.dot(stacked_inverse, stacked_panel, preferred_element_type=jnp.float32)
    negated = -my_pattern.astype(jnp.float32)
    signed = (partial_value.reshape(RB, B, supernodes, B) * negated[:, None, :, None]).reshape(
        local_rows, supernodes * B
    )
    return lax.psum_scatter(signed, "col", scatter_dimension=1, tiled=True)


def kernel(pattern_ref, t_ref, l_ref, out_ref, pat, t, m, acc,
           load_sem, z_send, c_send, f_send, t_send, t_recv, s_send, s_recv, o_send, o_recv, m_recv,
           ready):
    row = lax.axis_index("row")
    col = lax.axis_index("col")
    z, y = row // 2, row % 2
    x, k = col // 2, col % 2
    near = (z // 2 + x) % 2
    far = 1 - near
    core = (z + k) % 2
    half = B // 2
    z_next = z + 1 - 2 * (z % 2)

    def at(z_, y_, x_, k_):
        return (z_ * 2 + y_, x_ * 2 + k_)

    def slot(core_, side, y_, part=None):
        plane = core_ * 2 + side
        sem = (plane * 2 + y_) * 2
        if part is None:
            return m.at[plane, y_], m_recv.at[sem]
        return m.at[plane, y_, pl.ds(part * half, half)], m_recv.at[sem + part]

    def copy(src, dst, send, recv, where):
        return pltpu.make_async_remote_copy(
            src_ref=src, dst_ref=dst, send_sem=send, recv_sem=recv, device_id=where, device_id_type=MESH
        )

    x_mate = at(z, y, 1 - x, k)
    sibling = at(z, y, x, 1 - k)
    y_mate = at(z, 1 - y, x, k)
    z_far = at((z + 2) % 4, y, x, k)
    z_near = (at(z_next, y, x, k), at(z_next, 1 - y, x, k))

    barrier = pltpu.get_barrier_semaphore()
    mates = (z_far, y_mate, z_near[0], z_near[1], x_mate, sibling)
    is_later = (z < 2, y == 0, z % 2 == 0, z % 2 == 0, x == 0, k == 1)
    n_earlier = z // 2 + y + x + 2 * (z % 2) + 1 - k

    def greet(sem, where):
        pl.semaphore_signal(sem, inc=1, device_id=where, device_id_type=MESH)

    for where, later in zip(mates, is_later):
        @pl.when(later)
        def _(where=where):
            greet(barrier, where)

    load_pattern = pltpu.make_async_copy(pattern_ref, pat, load_sem.at[0])
    load_l = pltpu.make_async_copy(l_ref, m.at[core * 2 + near, y], load_sem.at[1])
    load_t = pltpu.make_async_copy(t_ref, t.at[0], load_sem.at[2])
    load_pattern.start()
    load_l.start()
    load_t.start()
    z_copies = []
    for part in range(2):
        dst, sem = slot(core, near, y, part)
        z_copies.append(copy(l_ref.at[pl.ds(part * half, half)], dst, z_send.at[part], sem, z_far))
    mine, mine_sem = slot(core, near, y)
    cross = copy(l_ref, mine, c_send.at[0], mine_sem, y_mate)
    direct = copy(l_ref, mine, c_send.at[1], mine_sem, z_near[0])
    passed, passed_sem = slot(1 - core, near, y)
    relay = copy(passed, passed, c_send.at[2], passed_sem, y_mate)
    t_rows = t.shape[1] // T_CHUNKS
    t_copies = []
    t_forwards = []
    for i in range(T_CHUNKS):
        rows = pl.ds(i * t_rows, t_rows)
        t_copies.append(copy(t_ref.at[rows], t.at[1, rows], t_send.at[i], t_recv.at[i], x_mate))
        t_forwards.append(copy(t.at[1, rows], t.at[3, rows], s_send.at[i], s_recv.at[i], sibling))
    t_sibling = copy(t_ref, t.at[2], o_send.at[0], o_recv.at[0], sibling)

    @pl.when(n_earlier > 0)
    def _():
        pl.semaphore_wait(barrier, n_earlier)

    groups = (z_copies, [cross], [direct], [], t_copies, [t_sibling])
    for i, (where, later) in enumerate(zip(mates, is_later)):
        @pl.when(jnp.logical_not(later))
        def _(i=i, where=where):
            greet(ready.at[i], where)
            for c in groups[i]:
                c.start()

    for i in (1, 2, 3, 4, 0, 5):
        @pl.when(is_later[i])
        def _(i=i):
            pl.semaphore_wait(ready.at[i], 1)
            for c in groups[i]:
                c.start()

    forwards = []

    def pass_panel(part):
        block, sem = slot(core, far, y, part)
        copy(block, block, f_send.at[0], sem, z_far).wait_recv()
        for i, where in enumerate((z_near[1], y_mate, z_near[0])):
            f = copy(block, block, f_send.at[part * 3 + i], sem, where)
            f.start()
            forwards.append(f)

    def pass_inverse(i):
        t_copies[i].wait_recv()
        t_forwards[i].start()

    pass_panel(0)
    relay.wait_recv()
    relay.start()
    pass_panel(1)

    def arrive(*place):
        block, sem = slot(*place)
        copy(block, block, f_send.at[0], sem, y_mate).wait_recv()

    def product(core_, side, y_):
        plane = core_ * 2 + side
        block_row = (2 * ((side + x) % 2) + (core_ + k) % 2) * 2 + y_
        keep = pat[x, block_row].astype(jnp.float32).astype(jnp.bfloat16)
        columns = pl.ds(pl.multiple_of(y_ * B, B), B)
        return jnp.dot(t[plane, :, columns], m[plane, y_] * keep, preferred_element_type=jnp.float32)

    def near_product(side):
        return product(0, side, 0) + product(0, side, 1) + product(1, side, 0) + product(1, side, 1)

    load_pattern.wait()
    load_l.wait()
    load_t.wait()
    arrive(core, near, 1 - y)
    arrive(1 - core, near, 1 - y)
    t_sibling.wait_recv()

    @pl.when(near == 0)
    def _():
        acc[...] = near_product(0)

    for i in range(T_CHUNKS):
        pass_inverse(i)
    for f in t_forwards:
        f.wait_recv()

    @pl.when(near == 1)
    def _():
        acc[...] = near_product(1)

    acc[...] += product(core, far, y)
    for part in range(2):
        arrive(core, far, 1 - y, part)
        arrive(1 - core, far, y, part)
    acc[...] += product(core, far, 1 - y) + product(1 - core, far, y)
    for part in range(2):
        arrive(1 - core, far, 1 - y, part)
    negated = -pat[x, row].astype(jnp.float32)
    out_ref[...] = (acc[...] + product(1 - core, far, 1 - y)) * negated

    for c in z_copies + [cross, direct, relay, t_sibling] + t_copies + t_forwards + forwards:
        c.wait_send()


def fused(trailing_inverse, l_panel, pattern):
    rows, depth = trailing_inverse.shape
    width = l_panel.shape[1]
    dma = pltpu.SemaphoreType.DMA
    operands = [pltpu.with_memory_space_constraint(v, pltpu.HBM) for v in (pattern.T, trailing_inverse, l_panel)]
    return pl.pallas_call(
        kernel,
        out_shape=jax.ShapeDtypeStruct((rows, width), jnp.float32),
        in_specs=[pl.BlockSpec(memory_space=pltpu.HBM)] * 3,
        out_specs=pl.BlockSpec(memory_space=pltpu.VMEM),
        scratch_shapes=[
            pltpu.SMEM(pattern.shape[::-1], jnp.int32),
            pltpu.VMEM((4, rows, depth), jnp.bfloat16),
            pltpu.VMEM((4, 2, B, width), jnp.bfloat16),
            pltpu.VMEM((rows, width), jnp.float32),
            dma((3,)),
            dma((2,)),
            dma((3,)),
            dma((6,)),
            dma((T_CHUNKS,)),
            dma((T_CHUNKS,)),
            dma((T_CHUNKS,)),
            dma((T_CHUNKS,)),
            dma((1,)),
            dma((1,)),
            dma((16,)),
            pltpu.SemaphoreType.REGULAR((6,)),
        ],
        compiler_params=pltpu.CompilerParams(
            collective_id=0, has_side_effects=True, vmem_limit_bytes=16 * 1024 * 1024
        ),
        cost_estimate=pl.CostEstimate(
            flops=2 * rows * 4 * depth * width, bytes_accessed=rows * depth * 4, transcendentals=0
        ),
    )(*operands)


def solution(mesh):
    whole_block = (mesh.shape["row"], mesh.shape["col"]) == (8, 4)
    return jax.shard_map(
        fused if whole_block else per_device,
        mesh=mesh,
        in_specs=(P("row", "col"), P("row", "col"), P()),
        out_specs=P("row", "col"),
        check_vma=False,
    )
```

```python
import functools

import jax
import jax.numpy as jnp
from jax import lax
from jax.experimental import pallas as pl
from jax.experimental.pallas import tpu as pltpu
from jax.sharding import PartitionSpec as P

B = 256
RB = 1
MESH = pl.DeviceIdType.MESH
T_CHUNKS = 4
PARTS = 4


def broadcast(value, axis, source):
    kept = jnp.where(lax.axis_index(axis) == source, value, 0).astype(value.dtype)
    return lax.psum(kept, axis)


def per_device(trailing_inverse, l_panel, pattern):
    grid_row = lax.axis_index("row")
    grid_col = lax.axis_index("col")
    ratio = lax.axis_size("row") // lax.axis_size("col")
    local_rows = l_panel.shape[0]
    supernodes = pattern.shape[1]
    my_pattern = lax.dynamic_slice_in_dim(pattern, grid_row * RB, RB, 0)
    full_row = lax.all_gather(l_panel, "col", axis=1, tiled=True)
    keep = my_pattern.astype(jnp.bfloat16)
    masked_row = (full_row.reshape(RB, B, supernodes, B) * keep[:, None, :, None]).reshape(
        local_rows, supernodes * B
    )
    arrived = []
    columns = []
    for turn in range(ratio):
        root = grid_col * ratio + turn
        piece = broadcast(masked_row, "row", root)
        inverse_cols = lax.dynamic_slice_in_dim(trailing_inverse, turn * local_rows, local_rows, 1)
        arrived.append(piece)
        columns.append(inverse_cols)
    stacked_panel = jnp.concatenate(arrived, 0)
    stacked_inverse = jnp.concatenate(columns, 1)
    partial_value = jnp.dot(stacked_inverse, stacked_panel, preferred_element_type=jnp.float32)
    negated = -my_pattern.astype(jnp.float32)
    signed = (partial_value.reshape(RB, B, supernodes, B) * negated[:, None, :, None]).reshape(
        local_rows, supernodes * B
    )
    return lax.psum_scatter(signed, "col", scatter_dimension=1, tiled=True)


def kernel(pattern_ref, t_ref, l_ref, out_ref, pat, t, m, acc,
           load_sem, z_send, c_send, f_send, t_send, t_recv, s_send, s_recv, o_send, o_recv, m_recv,
           ready):
    row = lax.axis_index("row")
    col = lax.axis_index("col")
    z, y = row // 2, row % 2
    x, k = col // 2, col % 2
    near = (z // 2 + x) % 2
    far = 1 - near
    core = (z + k) % 2
    piece = B // PARTS
    z_next = z + 1 - 2 * (z % 2)

    def at(z_, y_, x_, k_):
        return (z_ * 2 + y_, x_ * 2 + k_)

    def slot(core_, side, y_, part=None):
        plane = core_ * 2 + side
        sem = (plane * 2 + y_) * PARTS
        if part is None:
            return m.at[plane, y_], m_recv.at[sem]
        return m.at[plane, y_, pl.ds(part * piece, piece)], m_recv.at[sem + part]

    def copy(src, dst, send, recv, where):
        return pltpu.make_async_remote_copy(
            src_ref=src, dst_ref=dst, send_sem=send, recv_sem=recv, device_id=where, device_id_type=MESH
        )

    x_mate = at(z, y, 1 - x, k)
    sibling = at(z, y, x, 1 - k)
    y_mate = at(z, 1 - y, x, k)
    z_far = at((z + 2) % 4, y, x, k)
    z_near = (at(z_next, y, x, k), at(z_next, 1 - y, x, k))

    barrier = pltpu.get_barrier_semaphore()
    mates = (z_far, y_mate, z_near[0], z_near[1], x_mate, sibling)
    is_later = (z < 2, y == 0, z % 2 == 0, z % 2 == 0, x == 0, k == 1)
    n_earlier = z // 2 + y + x + 2 * (z % 2) + 1 - k

    def greet(sem, where):
        pl.semaphore_signal(sem, inc=1, device_id=where, device_id_type=MESH)

    for where, later in zip(mates, is_later):
        @pl.when(later)
        def _(where=where):
            greet(barrier, where)

    load_pattern = pltpu.make_async_copy(pattern_ref, pat, load_sem.at[0])
    load_l = pltpu.make_async_copy(l_ref, m.at[core * 2 + near, y], load_sem.at[1])
    load_t = pltpu.make_async_copy(t_ref, t.at[0], load_sem.at[2])
    load_pattern.start()
    load_l.start()
    load_t.start()
    z_copies = []
    for part in range(PARTS):
        dst, sem = slot(core, near, y, part)
        z_copies.append(copy(l_ref.at[pl.ds(part * piece, piece)], dst, z_send.at[part], sem, z_far))
    mine, mine_sem = slot(core, near, y)
    cross = copy(l_ref, mine, c_send.at[0], mine_sem, y_mate)
    direct = copy(l_ref, mine, c_send.at[1], mine_sem, z_near[0])
    diagonal = copy(l_ref, mine, c_send.at[2], mine_sem, z_near[1])
    t_rows = t.shape[1] // T_CHUNKS
    t_copies = []
    t_forwards = []
    for i in range(T_CHUNKS):
        rows = pl.ds(i * t_rows, t_rows)
        t_copies.append(copy(t_ref.at[rows], t.at[1, rows], t_send.at[i], t_recv.at[i], x_mate))
        t_forwards.append(copy(t.at[1, rows], t.at[3, rows], s_send.at[i], s_recv.at[i], sibling))
    t_sibling = copy(t_ref, t.at[2], o_send.at[0], o_recv.at[0], sibling)

    @pl.when(n_earlier > 0)
    def _():
        pl.semaphore_wait(barrier, n_earlier)

    groups = (z_copies, [cross], [direct], [diagonal], t_copies, [t_sibling])
    for i, (where, later) in enumerate(zip(mates, is_later)):
        @pl.when(jnp.logical_not(later))
        def _(i=i, where=where):
            greet(ready.at[i], where)
            for c in groups[i]:
                c.start()

    for i in (1, 2, 3, 4, 0, 5):
        @pl.when(is_later[i])
        def _(i=i):
            pl.semaphore_wait(ready.at[i], 1)
            for c in groups[i]:
                c.start()

    forwards = []

    def pass_panel(part):
        block, sem = slot(core, far, y, part)
        copy(block, block, f_send.at[0], sem, z_far).wait_recv()
        for i, where in enumerate((z_near[1], y_mate, z_near[0])):
            f = copy(block, block, f_send.at[part * 3 + i], sem, where)
            f.start()
            forwards.append(f)

    def pass_inverse(i):
        t_copies[i].wait_recv()
        t_forwards[i].start()

    for part in range(PARTS):
        pass_panel(part)

    def arrive(*place):
        block, sem = slot(*place)
        copy(block, block, f_send.at[0], sem, y_mate).wait_recv()

    def product(core_, side, y_):
        plane = core_ * 2 + side
        block_row = (2 * ((side + x) % 2) + (core_ + k) % 2) * 2 + y_
        keep = pat[x, block_row].astype(jnp.float32).astype(jnp.bfloat16)
        columns = pl.ds(pl.multiple_of(y_ * B, B), B)
        return jnp.dot(t[plane, :, columns], m[plane, y_] * keep, preferred_element_type=jnp.float32)

    def near_product(side):
        return product(0, side, 0) + product(0, side, 1) + product(1, side, 0) + product(1, side, 1)

    load_pattern.wait()
    load_l.wait()
    load_t.wait()
    arrive(core, near, 1 - y)
    arrive(1 - core, near, y)
    arrive(1 - core, near, 1 - y)
    t_sibling.wait_recv()

    @pl.when(near == 0)
    def _():
        acc[...] = near_product(0)

    for i in range(T_CHUNKS):
        pass_inverse(i)
    for f in t_forwards:
        f.wait_recv()

    @pl.when(near == 1)
    def _():
        acc[...] = near_product(1)

    acc[...] += product(core, far, y)
    for part in range(PARTS):
        arrive(core, far, 1 - y, part)
        arrive(1 - core, far, y, part)
    acc[...] += product(core, far, 1 - y) + product(1 - core, far, y)
    for part in range(PARTS):
        arrive(1 - core, far, 1 - y, part)
    negated = -pat[x, row].astype(jnp.float32)
    out_ref[...] = (acc[...] + product(1 - core, far, 1 - y)) * negated

    for c in z_copies + [cross, direct, diagonal, t_sibling] + t_copies + t_forwards + forwards:
        c.wait_send()


def fused(trailing_inverse, l_panel, pattern):
    rows, depth = trailing_inverse.shape
    width = l_panel.shape[1]
    dma = pltpu.SemaphoreType.DMA
    operands = [pltpu.with_memory_space_constraint(v, pltpu.HBM) for v in (pattern.T, trailing_inverse, l_panel)]
    return pl.pallas_call(
        kernel,
        out_shape=jax.ShapeDtypeStruct((rows, width), jnp.float32),
        in_specs=[pl.BlockSpec(memory_space=pltpu.HBM)] * 3,
        out_specs=pl.BlockSpec(memory_space=pltpu.VMEM),
        scratch_shapes=[
            pltpu.SMEM(pattern.shape[::-1], jnp.int32),
            pltpu.VMEM((4, rows, depth), jnp.bfloat16),
            pltpu.VMEM((4, 2, B, width), jnp.bfloat16),
            pltpu.VMEM((rows, width), jnp.float32),
            dma((3,)),
            dma((PARTS,)),
            dma((3,)),
            dma((3 * PARTS,)),
            dma((T_CHUNKS,)),
            dma((T_CHUNKS,)),
            dma((T_CHUNKS,)),
            dma((T_CHUNKS,)),
            dma((1,)),
            dma((1,)),
            dma((8 * PARTS,)),
            pltpu.SemaphoreType.REGULAR((6,)),
        ],
        compiler_params=pltpu.CompilerParams(
            collective_id=0, has_side_effects=True, vmem_limit_bytes=16 * 1024 * 1024
        ),
        cost_estimate=pl.CostEstimate(
            flops=2 * rows * 4 * depth * width, bytes_accessed=rows * depth * 4, transcendentals=0
        ),
    )(*operands)


def solution(mesh):
    whole_block = (mesh.shape["row"], mesh.shape["col"]) == (8, 4)
    return jax.shard_map(
        fused if whole_block else per_device,
        mesh=mesh,
        in_specs=(P("row", "col"), P("row", "col"), P()),
        out_specs=P("row", "col"),
        check_vma=False,
    )
```

```python
import functools

import jax
import jax.numpy as jnp
from jax import lax
from jax.experimental import pallas as pl
from jax.experimental.pallas import tpu as pltpu
from jax.sharding import PartitionSpec as P

B = 256
RB = 1
MESH = pl.DeviceIdType.MESH
T_CHUNKS = 4
PARTS = 4


def broadcast(value, axis, source):
    kept = jnp.where(lax.axis_index(axis) == source, value, 0).astype(value.dtype)
    return lax.psum(kept, axis)


def per_device(trailing_inverse, l_panel, pattern):
    grid_row = lax.axis_index("row")
    grid_col = lax.axis_index("col")
    ratio = lax.axis_size("row") // lax.axis_size("col")
    local_rows = l_panel.shape[0]
    supernodes = pattern.shape[1]
    my_pattern = lax.dynamic_slice_in_dim(pattern, grid_row * RB, RB, 0)
    full_row = lax.all_gather(l_panel, "col", axis=1, tiled=True)
    keep = my_pattern.astype(jnp.bfloat16)
    masked_row = (full_row.reshape(RB, B, supernodes, B) * keep[:, None, :, None]).reshape(
        local_rows, supernodes * B
    )
    arrived = []
    columns = []
    for turn in range(ratio):
        root = grid_col * ratio + turn
        piece = broadcast(masked_row, "row", root)
        inverse_cols = lax.dynamic_slice_in_dim(trailing_inverse, turn * local_rows, local_rows, 1)
        arrived.append(piece)
        columns.append(inverse_cols)
    stacked_panel = jnp.concatenate(arrived, 0)
    stacked_inverse = jnp.concatenate(columns, 1)
    partial_value = jnp.dot(stacked_inverse, stacked_panel, preferred_element_type=jnp.float32)
    negated = -my_pattern.astype(jnp.float32)
    signed = (partial_value.reshape(RB, B, supernodes, B) * negated[:, None, :, None]).reshape(
        local_rows, supernodes * B
    )
    return lax.psum_scatter(signed, "col", scatter_dimension=1, tiled=True)


def kernel(pattern_ref, t_ref, l_ref, out_ref, pat, t, m, acc,
           load_sem, z_send, c_send, f_send, t_send, t_recv, s_send, s_recv, o_send, o_recv, m_recv,
           ready):
    row = lax.axis_index("row")
    col = lax.axis_index("col")
    z, y = row // 2, row % 2
    x, k = col // 2, col % 2
    near = (z // 2 + x) % 2
    far = 1 - near
    core = (z + k) % 2
    piece = B // PARTS
    z_next = z + 1 - 2 * (z % 2)

    def at(z_, y_, x_, k_):
        return (z_ * 2 + y_, x_ * 2 + k_)

    def slot(core_, side, y_, part=None):
        plane = core_ * 2 + side
        sem = (plane * 2 + y_) * PARTS
        if part is None:
            return m.at[plane, y_], m_recv.at[sem]
        return m.at[plane, y_, pl.ds(part * piece, piece)], m_recv.at[sem + part]

    def copy(src, dst, send, recv, where):
        return pltpu.make_async_remote_copy(
            src_ref=src, dst_ref=dst, send_sem=send, recv_sem=recv, device_id=where, device_id_type=MESH
        )

    x_mate = at(z, y, 1 - x, k)
    sibling = at(z, y, x, 1 - k)
    y_mate = at(z, 1 - y, x, k)
    z_far = at((z + 2) % 4, y, x, k)
    z_near = (at(z_next, y, x, k), at(z_next, 1 - y, x, k))

    barrier = pltpu.get_barrier_semaphore()
    mates = (z_far, y_mate, z_near[0], z_near[1], x_mate, sibling)
    is_later = (z < 2, y == 0, z % 2 == 0, z % 2 == 0, x == 0, k == 1)
    n_earlier = z // 2 + y + x + 2 * (z % 2) + 1 - k

    def greet(sem, where):
        pl.semaphore_signal(sem, inc=1, device_id=where, device_id_type=MESH)

    for where, later in zip(mates, is_later):
        @pl.when(later)
        def _(where=where):
            greet(barrier, where)

    load_pattern = pltpu.make_async_copy(pattern_ref, pat, load_sem.at[0])
    load_l = pltpu.make_async_copy(l_ref, m.at[core * 2 + near, y], load_sem.at[1])
    load_t = pltpu.make_async_copy(t_ref, t.at[0], load_sem.at[2])
    load_pattern.start()
    load_l.start()
    load_t.start()
    z_copies = []
    for part in range(PARTS):
        dst, sem = slot(core, near, y, part)
        z_copies.append(copy(l_ref.at[pl.ds(part * piece, piece)], dst, z_send.at[part], sem, z_far))
    mine, mine_sem = slot(core, near, y)
    cross = copy(l_ref, mine, c_send.at[0], mine_sem, y_mate)
    direct = copy(l_ref, mine, c_send.at[1], mine_sem, z_near[0])
    diagonal = copy(l_ref, mine, c_send.at[2], mine_sem, z_near[1])
    t_rows = t.shape[1] // T_CHUNKS
    t_copies = []
    t_forwards = []
    for i in range(T_CHUNKS):
        rows = pl.ds(i * t_rows, t_rows)
        t_copies.append(copy(t_ref.at[rows], t.at[1, rows], t_send.at[i], t_recv.at[i], x_mate))
        t_forwards.append(copy(t.at[1, rows], t.at[3, rows], s_send.at[i], s_recv.at[i], sibling))
    t_sibling = copy(t_ref, t.at[2], o_send.at[0], o_recv.at[0], sibling)

    @pl.when(n_earlier > 0)
    def _():
        pl.semaphore_wait(barrier, n_earlier)

    groups = (z_copies, [cross], [direct], [diagonal], t_copies, [t_sibling])
    for i, (where, later) in enumerate(zip(mates, is_later)):
        @pl.when(jnp.logical_not(later))
        def _(i=i, where=where):
            greet(ready.at[i], where)
            if i not in (2, 3):
                for c in groups[i]:
                    c.start()

    def start_later(*which):
        for i in which:
            @pl.when(is_later[i])
            def _(i=i):
                pl.semaphore_wait(ready.at[i], 1)
                for c in groups[i]:
                    c.start()

    def start_near():
        for i in (2, 3):
            @pl.when(is_later[i])
            def _(i=i):
                pl.semaphore_wait(ready.at[i], 1)

            for c in groups[i]:
                c.start()

    start_later(1)

    @pl.when(z < 2)
    def _():
        start_near()

    start_later(4, 0, 5)

    @pl.when(z >= 2)
    def _():
        for c in z_copies:
            c.wait_send()
        start_near()

    forwards = []

    def pass_panel(part):
        block, sem = slot(core, far, y, part)
        copy(block, block, f_send.at[0], sem, z_far).wait_recv()
        for i, where in enumerate((z_near[1], y_mate, z_near[0])):
            f = copy(block, block, f_send.at[part * 3 + i], sem, where)
            f.start()
            forwards.append(f)

    def pass_inverse(i):
        t_copies[i].wait_recv()
        t_forwards[i].start()

    for part in range(PARTS):
        pass_panel(part)

    def arrive(*place):
        block, sem = slot(*place)
        copy(block, block, f_send.at[0], sem, y_mate).wait_recv()

    def product(core_, side, y_):
        plane = core_ * 2 + side
        block_row = (2 * ((side + x) % 2) + (core_ + k) % 2) * 2 + y_
        keep = pat[x, block_row].astype(jnp.float32).astype(jnp.bfloat16)
        columns = pl.ds(pl.multiple_of(y_ * B, B), B)
        return jnp.dot(t[plane, :, columns], m[plane, y_] * keep, preferred_element_type=jnp.float32)

    def near_product(side):
        return product(0, side, 0) + product(0, side, 1) + product(1, side, 0) + product(1, side, 1)

    load_pattern.wait()
    load_l.wait()
    load_t.wait()
    arrive(core, near, 1 - y)
    arrive(1 - core, near, y)
    arrive(1 - core, near, 1 - y)
    t_sibling.wait_recv()

    @pl.when(near == 0)
    def _():
        acc[...] = near_product(0)

    for i in range(T_CHUNKS):
        pass_inverse(i)
    for f in t_forwards:
        f.wait_recv()

    @pl.when(near == 1)
    def _():
        acc[...] = near_product(1)

    acc[...] += product(core, far, y)
    for part in range(PARTS):
        arrive(core, far, 1 - y, part)
        arrive(1 - core, far, y, part)
    acc[...] += product(core, far, 1 - y) + product(1 - core, far, y)
    for part in range(PARTS):
        arrive(1 - core, far, 1 - y, part)
    negated = -pat[x, row].astype(jnp.float32)
    out_ref[...] = (acc[...] + product(1 - core, far, 1 - y)) * negated

    @pl.when(z < 2)
    def _():
        for c in z_copies:
            c.wait_send()

    for c in [cross, direct, diagonal, t_sibling] + t_copies + t_forwards + forwards:
        c.wait_send()


def fused(trailing_inverse, l_panel, pattern):
    rows, depth = trailing_inverse.shape
    width = l_panel.shape[1]
    dma = pltpu.SemaphoreType.DMA
    operands = [pltpu.with_memory_space_constraint(v, pltpu.HBM) for v in (pattern.T, trailing_inverse, l_panel)]
    return pl.pallas_call(
        kernel,
        out_shape=jax.ShapeDtypeStruct((rows, width), jnp.float32),
        in_specs=[pl.BlockSpec(memory_space=pltpu.HBM)] * 3,
        out_specs=pl.BlockSpec(memory_space=pltpu.VMEM),
        scratch_shapes=[
            pltpu.SMEM(pattern.shape[::-1], jnp.int32),
            pltpu.VMEM((4, rows, depth), jnp.bfloat16),
            pltpu.VMEM((4, 2, B, width), jnp.bfloat16),
            pltpu.VMEM((rows, width), jnp.float32),
            dma((3,)),
            dma((PARTS,)),
            dma((3,)),
            dma((3 * PARTS,)),
            dma((T_CHUNKS,)),
            dma((T_CHUNKS,)),
            dma((T_CHUNKS,)),
            dma((T_CHUNKS,)),
            dma((1,)),
            dma((1,)),
            dma((8 * PARTS,)),
            pltpu.SemaphoreType.REGULAR((6,)),
        ],
        compiler_params=pltpu.CompilerParams(
            collective_id=0, has_side_effects=True, vmem_limit_bytes=16 * 1024 * 1024
        ),
        cost_estimate=pl.CostEstimate(
            flops=2 * rows * 4 * depth * width, bytes_accessed=rows * depth * 4, transcendentals=0
        ),
    )(*operands)


def solution(mesh):
    whole_block = (mesh.shape["row"], mesh.shape["col"]) == (8, 4)
    return jax.shard_map(
        fused if whole_block else per_device,
        mesh=mesh,
        in_specs=(P("row", "col"), P("row", "col"), P()),
        out_specs=P("row", "col"),
        check_vma=False,
    )
```

```python
import functools

import jax
import jax.numpy as jnp
from jax import lax
from jax.experimental import pallas as pl
from jax.experimental.pallas import tpu as pltpu
from jax.sharding import PartitionSpec as P

B = 256
RB = 1
MESH = pl.DeviceIdType.MESH
T_CHUNKS = 2
PARTS = 4


def broadcast(value, axis, source):
    kept = jnp.where(lax.axis_index(axis) == source, value, 0).astype(value.dtype)
    return lax.psum(kept, axis)


def per_device(trailing_inverse, l_panel, pattern):
    grid_row = lax.axis_index("row")
    grid_col = lax.axis_index("col")
    ratio = lax.axis_size("row") // lax.axis_size("col")
    local_rows = l_panel.shape[0]
    supernodes = pattern.shape[1]
    my_pattern = lax.dynamic_slice_in_dim(pattern, grid_row * RB, RB, 0)
    full_row = lax.all_gather(l_panel, "col", axis=1, tiled=True)
    keep = my_pattern.astype(jnp.bfloat16)
    masked_row = (full_row.reshape(RB, B, supernodes, B) * keep[:, None, :, None]).reshape(
        local_rows, supernodes * B
    )
    arrived = []
    columns = []
    for turn in range(ratio):
        root = grid_col * ratio + turn
        piece = broadcast(masked_row, "row", root)
        inverse_cols = lax.dynamic_slice_in_dim(trailing_inverse, turn * local_rows, local_rows, 1)
        arrived.append(piece)
        columns.append(inverse_cols)
    stacked_panel = jnp.concatenate(arrived, 0)
    stacked_inverse = jnp.concatenate(columns, 1)
    partial_value = jnp.dot(stacked_inverse, stacked_panel, preferred_element_type=jnp.float32)
    negated = -my_pattern.astype(jnp.float32)
    signed = (partial_value.reshape(RB, B, supernodes, B) * negated[:, None, :, None]).reshape(
        local_rows, supernodes * B
    )
    return lax.psum_scatter(signed, "col", scatter_dimension=1, tiled=True)


def kernel(pattern_ref, t_ref, l_ref, out_ref, pat, t, m, acc,
           load_sem, z_send, c_send, f_send, t_send, t_recv, s_send, s_recv, o_send, o_recv, m_recv,
           ready):
    row = lax.axis_index("row")
    col = lax.axis_index("col")
    z, y = row // 2, row % 2
    x, k = col // 2, col % 2
    near = (z // 2 + x) % 2
    far = 1 - near
    core = (z + k) % 2
    piece = B // PARTS
    z_next = z + 1 - 2 * (z % 2)

    def at(z_, y_, x_, k_):
        return (z_ * 2 + y_, x_ * 2 + k_)

    def slot(core_, side, y_, part=None):
        plane = core_ * 2 + side
        sem = (plane * 2 + y_) * PARTS
        if part is None:
            return m.at[plane, y_], m_recv.at[sem]
        return m.at[plane, y_, pl.ds(part * piece, piece)], m_recv.at[sem + part]

    def copy(src, dst, send, recv, where):
        return pltpu.make_async_remote_copy(
            src_ref=src, dst_ref=dst, send_sem=send, recv_sem=recv, device_id=where, device_id_type=MESH
        )

    x_mate = at(z, y, 1 - x, k)
    sibling = at(z, y, x, 1 - k)
    y_mate = at(z, 1 - y, x, k)
    z_far = at((z + 2) % 4, y, x, k)
    z_near = (at(z_next, y, x, k), at(z_next, 1 - y, x, k))

    barrier = pltpu.get_barrier_semaphore()
    mates = (z_far, y_mate, z_near[0], z_near[1], x_mate, sibling)
    is_later = (z < 2, y == 0, z % 2 == 0, z % 2 == 0, x == 0, k == 1)
    n_earlier = z // 2 + y + x + 2 * (z % 2) + 1 - k

    def greet(sem, where):
        pl.semaphore_signal(sem, inc=1, device_id=where, device_id_type=MESH)

    for where, later in zip(mates, is_later):
        @pl.when(later)
        def _(where=where):
            greet(barrier, where)

    load_pattern = pltpu.make_async_copy(pattern_ref, pat, load_sem.at[0])
    load_l = pltpu.make_async_copy(l_ref, m.at[core * 2 + near, y], load_sem.at[1])
    load_t = pltpu.make_async_copy(t_ref, t.at[0], load_sem.at[2])
    load_pattern.start()
    load_l.start()
    load_t.start()
    z_copies = []
    for part in range(PARTS):
        dst, sem = slot(core, near, y, part)
        z_copies.append(copy(l_ref.at[pl.ds(part * piece, piece)], dst, z_send.at[part], sem, z_far))
    mine, mine_sem = slot(core, near, y)
    cross = copy(l_ref, mine, c_send.at[0], mine_sem, y_mate)
    direct = copy(l_ref, mine, c_send.at[1], mine_sem, z_near[0])
    diagonal = copy(l_ref, mine, c_send.at[2], mine_sem, z_near[1])
    t_rows = t.shape[1] // T_CHUNKS
    t_copies = []
    t_forwards = []
    for i in range(T_CHUNKS):
        rows = pl.ds(i * t_rows, t_rows)
        t_copies.append(copy(t_ref.at[rows], t.at[1, rows], t_send.at[i], t_recv.at[i], x_mate))
        t_forwards.append(copy(t.at[1, rows], t.at[3, rows], s_send.at[i], s_recv.at[i], sibling))
    t_sibling = copy(t_ref, t.at[2], o_send.at[0], o_recv.at[0], sibling)

    @pl.when(n_earlier > 0)
    def _():
        pl.semaphore_wait(barrier, n_earlier)

    groups = (z_copies, [cross], [direct], [diagonal], t_copies, [t_sibling])
    for i, (where, later) in enumerate(zip(mates, is_later)):
        @pl.when(jnp.logical_not(later))
        def _(i=i, where=where):
            greet(ready.at[i], where)
            for c in groups[i]:
                c.start()

    for i in (1, 2, 3, 4, 0, 5):
        @pl.when(is_later[i])
        def _(i=i):
            pl.semaphore_wait(ready.at[i], 1)
            for c in groups[i]:
                c.start()

    forwards = []

    def pass_panel(part):
        block, sem = slot(core, far, y, part)
        copy(block, block, f_send.at[0], sem, z_far).wait_recv()
        for i, where in enumerate((z_near[1], y_mate, z_near[0])):
            f = copy(block, block, f_send.at[part * 3 + i], sem, where)
            f.start()
            forwards.append(f)

    def pass_inverse(i):
        t_copies[i].wait_recv()
        t_forwards[i].start()

    for part in range(PARTS):
        pass_panel(part)

    def arrive(*place):
        block, sem = slot(*place)
        copy(block, block, f_send.at[0], sem, y_mate).wait_recv()

    def product(core_, side, y_):
        plane = core_ * 2 + side
        block_row = (2 * ((side + x) % 2) + (core_ + k) % 2) * 2 + y_
        keep = pat[x, block_row].astype(jnp.float32).astype(jnp.bfloat16)
        columns = pl.ds(pl.multiple_of(y_ * B, B), B)
        return jnp.dot(t[plane, :, columns], m[plane, y_] * keep, preferred_element_type=jnp.float32)

    def near_product(side):
        return product(0, side, 0) + product(0, side, 1) + product(1, side, 0) + product(1, side, 1)

    load_pattern.wait()
    load_l.wait()
    load_t.wait()
    arrive(core, near, 1 - y)
    arrive(1 - core, near, y)
    arrive(1 - core, near, 1 - y)
    t_sibling.wait_recv()

    @pl.when(near == 0)
    def _():
        acc[...] = near_product(0)

    for i in range(T_CHUNKS):
        pass_inverse(i)
    for f in t_forwards:
        f.wait_recv()

    @pl.when(near == 1)
    def _():
        acc[...] = near_product(1)

    acc[...] += product(core, far, y)
    for part in range(PARTS):
        arrive(core, far, 1 - y, part)
        arrive(1 - core, far, y, part)
    acc[...] += product(core, far, 1 - y) + product(1 - core, far, y)
    for part in range(PARTS):
        arrive(1 - core, far, 1 - y, part)
    negated = -pat[x, row].astype(jnp.float32)
    out_ref[...] = (acc[...] + product(1 - core, far, 1 - y)) * negated

    for c in z_copies + [cross, direct, diagonal, t_sibling] + t_copies + t_forwards + forwards:
        c.wait_send()


def fused(trailing_inverse, l_panel, pattern):
    rows, depth = trailing_inverse.shape
    width = l_panel.shape[1]
    dma = pltpu.SemaphoreType.DMA
    operands = [pltpu.with_memory_space_constraint(v, pltpu.HBM) for v in (pattern.T, trailing_inverse, l_panel)]
    return pl.pallas_call(
        kernel,
        out_shape=jax.ShapeDtypeStruct((rows, width), jnp.float32),
        in_specs=[pl.BlockSpec(memory_space=pltpu.HBM)] * 3,
        out_specs=pl.BlockSpec(memory_space=pltpu.VMEM),
        scratch_shapes=[
            pltpu.SMEM(pattern.shape[::-1], jnp.int32),
            pltpu.VMEM((4, rows, depth), jnp.bfloat16),
            pltpu.VMEM((4, 2, B, width), jnp.bfloat16),
            pltpu.VMEM((rows, width), jnp.float32),
            dma((3,)),
            dma((PARTS,)),
            dma((3,)),
            dma((3 * PARTS,)),
            dma((T_CHUNKS,)),
            dma((T_CHUNKS,)),
            dma((T_CHUNKS,)),
            dma((T_CHUNKS,)),
            dma((1,)),
            dma((1,)),
            dma((8 * PARTS,)),
            pltpu.SemaphoreType.REGULAR((6,)),
        ],
        compiler_params=pltpu.CompilerParams(
            collective_id=0, has_side_effects=True, vmem_limit_bytes=16 * 1024 * 1024
        ),
        cost_estimate=pl.CostEstimate(
            flops=2 * rows * 4 * depth * width, bytes_accessed=rows * depth * 4, transcendentals=0
        ),
    )(*operands)


def solution(mesh):
    whole_block = (mesh.shape["row"], mesh.shape["col"]) == (8, 4)
    return jax.shard_map(
        fused if whole_block else per_device,
        mesh=mesh,
        in_specs=(P("row", "col"), P("row", "col"), P()),
        out_specs=P("row", "col"),
        check_vma=False,
    )
```
